256 devices in a mesh: image: 64 (over z, x, core), tensor: 4 (over y).
Axes of the slice: x: 4, y: 4, z: 8, core: 2. Of those that a mesh axis runs over, the one named last changes fastest.
Arguments:
- queries: bfloat16 [1024, 8192], P('image', 'tensor')
- query_gain: bfloat16 [128], replicated, may hold values from 0.099609375 to 1.8984375
- keys: bfloat16 [64, 6404, 1024], P('image', None, 'tensor')
- values: bfloat16 [64, 6404, 1024], P('image', None, 'tensor'), may hold values from -6 to 6
- out_weight: bfloat16 [8192, 8192], P('tensor', 'image'), may hold values from -0.0625 to 0.0625
- gate: float32 [1], replicated, may hold values from 0.5 to 1.5
- doc_images: int32 [8], replicated, may hold values from 1 to 24, 64 in all
- image_owner: int32 [64], replicated, may hold values from 0 to 63, each once
- image_start: int32 [64], replicated, may hold values from 0 to 159
Outputs:
- gated: bfloat16 [1024, 8192], P('tensor', 'image')
The draws below stay inside these ranges and needn't reach their ends.
Inputs may be any that keep to these rules, and one draw needn't show every extreme that they name: image_owner is a permutation of the 64 storage slots. `doc_images`: each document has at least one image; the counts sum to 64 and the largest is exactly 24. `image_start`: an image whose start is 128 or more is seen by no token of the span.
All inputs are finite; a program needn't handle non-finite values.
Results may differ from the reference program's by a relative error of at most 0.017.
Values may be sent and summed in bfloat16 or wider, within the bound.
A program may use at most 128 MiB of HBM per device.

```python
import math
import jax
import jax.numpy as jnp
import numpy as np
from jax import lax

D = 8192
HQ = 64
KVH = 8
HD = 128
IMG_TOK = 6404
DOCS = 8
SPAN = 128
TEXT = 1024
IMAGES = 64
MOST_IMG = 24


def draw_queries(key, part):
    key = jax.random.fold_in(key, 11)
    base = jax.random.normal(key, (TEXT, HQ * HD), jnp.float32)
    return jnp.clip(base, -30.0, 30.0).astype(jnp.bfloat16)


def draw_keys(key, part):
    key = jax.random.fold_in(key, 12)
    base = jnp.clip(jax.random.normal(key, (IMAGES, IMG_TOK, KVH * HD), jnp.float32), -6.0, 6.0)
    return base.astype(jnp.bfloat16)


def with_ends(values, rng, least, top_value):
    longest = values.shape.index(max(values.shape))
    spots = []
    for shift in (0, 1):
        where = [jax.random.randint(jax.random.fold_in(rng, axis), (), 0, length) for axis, length in enumerate(values.shape)]
        where[longest] = (where[longest] + shift) % values.shape[longest]
        spots.append(tuple(where))
    return values.at[spots[0]].set(least).at[spots[1]].set(top_value)


def block_levels(key, dims, pieces, low, top_value):
    def one(position, parts):
        heights = jax.random.uniform(jax.random.fold_in(jax.random.fold_in(key, 6), position), (parts,), jnp.float32, low / len(pieces), top_value / len(pieces))
        return jnp.repeat(jnp.exp(heights), dims[position] // parts).reshape((-1,) + (1,) * (len(dims) - position - 1))

    loudness = one(*pieces[0])
    for cut in pieces[1:]:
        loudness = loudness * one(*cut)
    return loudness


def split_up(amount, total, bound, skew):
    weights = [(1 << 20) // math.isqrt(standing ** skew) + 1 for standing in range(2, amount + 1)]
    surplus, holding = total - bound - (amount - 1), [1] * (amount - 1)
    while surplus > 0:
        candidates = [i for i in range(amount - 1) if holding[i] < bound]
        whole, left = sum([weights[i] for i in candidates]), surplus
        for i in candidates:
            extra = min(bound - holding[i], max(1, left * weights[i] // whole), surplus)
            holding[i] = holding[i] + extra
            surplus = surplus - extra
    return np.array([bound] + holding)


def uneven(rng, amount, total, reach, slope):
    if amount == 2:
        one = jax.random.randint(rng, (), max(1, total - reach), min(reach, total - 1) + 1)
        return jnp.stack([one, total - one])
    sizes = jnp.asarray(split_up(amount, total, reach, slope), jnp.int32)
    twos = (amount - 1) // 2
    giver, receiver = sizes[1:1 + 2 * twos:2], sizes[2:2 + 2 * twos:2]
    room = jnp.minimum(giver - 1, reach - receiver)
    passed = jax.random.randint(jax.random.fold_in(rng, 1), (twos,), 0, 1 << 20) % (room + 1)
    sizes = sizes.at[1:1 + 2 * twos:2].set(giver - passed).at[2:2 + 2 * twos:2].set(receiver + passed)
    return sizes[jax.random.permutation(jax.random.fold_in(rng, 2), amount)]


def bell_draw(key, extent, scale, most, cuts=(), kind=jnp.bfloat16):
    factor_of = block_levels(key, extent, cuts, -0.22, 0.18) if cuts else 1.0
    result = jax.random.normal(key, extent, jnp.float32) * scale * factor_of
    return jnp.minimum(jnp.maximum(result, -most), most).astype(kind)


def setup_inputs(seed: int = 0) -> dict:
    key_list = jax.random.split(jax.random.key(seed), 10)
    queries = draw_queries(jax.random.fold_in(key_list[9], 71), 0)
    query_gain = jnp.clip(1.0 + 0.18 * jax.random.normal(key_list[1], (HD,), jnp.float32), 0.099609375, 1.8984375).astype(jnp.bfloat16)
    keys = draw_keys(jax.random.fold_in(key_list[9], 71), 0)
    values = bell_draw(key_list[3], (IMAGES, IMG_TOK, KVH * HD), 1.0, 6.0, ((0, 64), (2, 4)))
    out_weight = bell_draw(key_list[4], (HQ * HD, D), (HQ * HD) ** -0.5, 0.0625, ((0, 4), (1, 64)))
    gate = jnp.clip(jax.random.uniform(key_list[5], (1,), jnp.float32, 0.5, 1.5), 0.5, 1.5)
    doc_images = uneven(key_list[6], DOCS, IMAGES, MOST_IMG, 2).astype(jnp.int32)
    image_owner = jax.random.permutation(key_list[7], IMAGES).astype(jnp.int32)
    image_start = with_ends(jax.random.randint(key_list[8], (IMAGES,), 0, SPAN + SPAN // 4), jax.random.fold_in(key_list[8], 1), 0, (SPAN + SPAN // 4) - 1).astype(jnp.int32)
    return {"queries": queries, "query_gain": query_gain, "keys": keys, "values": values, "out_weight": out_weight, "gate": gate, "doc_images": doc_images, "image_owner": image_owner, "image_start": image_start}


def image_partials(rows, key_image, value_image):
    group = HQ // KVH
    scale = 1.0 / math.sqrt(HD)

    def one_group(index):
        block = lax.dynamic_slice_in_dim(rows, index * group, group, 1).reshape(SPAN * group, HD)
        key_block = lax.dynamic_slice_in_dim(key_image, index * HD, HD, 1)
        value_block = lax.dynamic_slice_in_dim(value_image, index * HD, HD, 1)
        scores = jnp.dot(key_block, block.T, preferred_element_type=jnp.float32) * scale
        peak = lax.optimization_barrier(jnp.max(scores, axis=0))
        weights = jnp.exp(scores - peak[None, :]).astype(jnp.bfloat16)
        acc = jnp.dot(weights.T, value_block, preferred_element_type=jnp.float32)
        total = lax.optimization_barrier(jnp.sum(weights, axis=0, dtype=jnp.float32))
        return (acc, peak, total)
    accs, peaks, totals = lax.map(one_group, jnp.arange(KVH, dtype=jnp.int32))
    accs = jnp.transpose(accs.reshape(KVH, SPAN, group, HD), (1, 0, 2, 3)).reshape(SPAN, HQ, HD)
    peaks = jnp.transpose(peaks.reshape(KVH, SPAN, group), (1, 0, 2)).reshape(SPAN, HQ)
    totals = jnp.transpose(totals.reshape(KVH, SPAN, group), (1, 0, 2)).reshape(SPAN, HQ)
    return (accs, peaks, totals)

def reference(queries, query_gain, keys, values, out_weight, gate, doc_images, image_owner, image_start):
    shaped = queries.astype(jnp.float32).reshape(TEXT, HQ, HD)
    normed = (shaped * lax.rsqrt(lax.optimization_barrier(jnp.mean(shaped * shaped, axis=2, keepdims=True)) + 1e-05) * query_gain.astype(jnp.float32)).astype(jnp.bfloat16)
    ends = jnp.cumsum(doc_images).astype(jnp.int32)
    ordinal = jnp.arange(IMAGES, dtype=jnp.int32)
    image_doc = lax.optimization_barrier(jnp.sum((ordinal[:, None] >= ends[None, :]).astype(jnp.int32), axis=1)).astype(jnp.int32)
    positions = jnp.arange(SPAN, dtype=jnp.int32)

    def step(carry, item):
        top, numer, denom = carry
        doc, owner, start = item
        first = (doc * SPAN).astype(jnp.int32)
        rows = lax.dynamic_slice_in_dim(normed, first, SPAN, 0)
        key_image = lax.dynamic_index_in_dim(keys, owner.astype(jnp.int32), 0, keepdims=False)
        value_image = lax.dynamic_index_in_dim(values, owner.astype(jnp.int32), 0, keepdims=False)
        accs, peaks, totals = image_partials(rows, key_image, value_image)
        valid = (positions >= start)[:, None]
        masked_peak = jnp.where(valid, peaks, jnp.float32(-1e+30))
        top_rows = lax.dynamic_slice_in_dim(top, first, SPAN, 0)
        numer_rows = lax.dynamic_slice_in_dim(numer, first, SPAN, 0)
        denom_rows = lax.dynamic_slice_in_dim(denom, first, SPAN, 0)
        new_top = jnp.maximum(top_rows, masked_peak)
        old_factor = jnp.exp(top_rows - new_top)
        factor = jnp.where(valid, jnp.exp(masked_peak - new_top), jnp.float32(0.0))
        numer_rows = numer_rows * old_factor[:, :, None] + factor[:, :, None] * accs
        denom_rows = denom_rows * old_factor + factor * totals
        top = lax.dynamic_update_slice_in_dim(top, new_top, first, 0)
        numer = lax.dynamic_update_slice_in_dim(numer, numer_rows, first, 0)
        denom = lax.dynamic_update_slice_in_dim(denom, denom_rows, first, 0)
        return ((top, numer, denom), None)
    start_carry = (jnp.full((TEXT, HQ), -1e+30, jnp.float32), jnp.zeros((TEXT, HQ, HD), jnp.float32), jnp.zeros((TEXT, HQ), jnp.float32))
    (top, numer, denom), unused = lax.scan(step, start_carry, (image_doc, image_owner, image_start))
    attended = (numer / jnp.maximum(denom, 1.0)[:, :, None]).astype(jnp.bfloat16).reshape(TEXT, HQ * HD)
    product = jnp.dot(attended, out_weight, preferred_element_type=jnp.float32)
    return (jnp.tanh(gate[0]) * product).astype(jnp.bfloat16)
```

```python
import functools
import math

import jax
import jax.numpy as jnp
from jax import lax
from jax.experimental import pallas as pl
from jax.experimental.pallas import tpu as pltpu
from jax.sharding import PartitionSpec as P

HD = 128
ROWS = 16
PLANES = 8
PEERS = 8
CHUNKS = 4
HEADS = 4
WIDE = HEADS * HD
BLOCK = WIDE + 128
TOK = 6404
BODY = 6400
NONE = -1e30
SEEN = -1e29
MESH = pl.DeviceIdType.MESH
NT = (((1,), (1,)), ((), ()))


def kernel(
    q_ref, gain_ref, k_hbm, v_hbm, w_hbm, gate_ref, docs_ref, owner_ref, start_ref,
    out_ref,
    k_ref, v_ref, vt_ref, kt_ref, w_ref,
    q1, sel, q2, obuf, m3, dbuf, m4, att, ag, part, partb, rs,
    ksem, vsem, wsem, wsend, wrecv,
    s1s, s1r, s2s, s2r, s3s, s3r, s4s, s4r, s5s, s5r, s5cs, s5cr, s6s, s6r, s7s, s7r,
):
    me = lax.axis_index("image")
    y = lax.axis_index("tensor")
    z, p = me // PEERS, lax.rem(me, PEERS)
    x, core = p // 2, lax.rem(p, 2)
    other = 1 - core

    def image_id(zz, pp):
        return zz * PEERS + pp

    def remote(src, dst, ssem, rsem, img, yy=None):
        return pltpu.make_async_remote_copy(
            src_ref=src, dst_ref=dst, send_sem=ssem, recv_sem=rsem,
            device_id=(img, y if yy is None else yy), device_id_type=MESH,
        )

    k_copy = pltpu.make_async_copy(k_hbm.at[0], k_ref, ksem)
    v_copy = pltpu.make_async_copy(v_hbm.at[0], v_ref, vsem)
    w_copy = pltpu.make_async_copy(w_hbm.at[:, core], w_ref.at[core], wsem)
    v_copy.start()
    k_copy.start()
    w_copy.start()

    barrier = pltpu.get_barrier_semaphore()

    def greet(img, yy):
        pl.semaphore_signal(barrier, inc=1, device_id=(img, yy), device_id_type=MESH)

    for j in range(1, PLANES):
        zz = lax.rem(z + j, PLANES)
        greet(image_id(zz, p), y)
        greet(image_id(zz, x * 2 + other), y)
    for d in range(1, PEERS):
        greet(image_id(z, lax.rem(p + d, PEERS)), y)
    for j in range(1, 4):
        yy = lax.rem(y + j, 4)
        greet(me, yy)
        greet(image_id(z, x * 2 + other), yy)

    gain = gain_ref[...].astype(jnp.float32) * (math.log2(math.e) / math.sqrt(HD))
    for h in range(CHUNKS * HEADS):
        rows = q_ref[:, h * HD : (h + 1) * HD].astype(jnp.float32)
        inv = lax.rsqrt(jnp.mean(rows * rows, axis=1, keepdims=True) + 1e-05)
        lo = (h % HEADS) * HD
        q1[h // HEADS, 0, :, lo : lo + HD] = (rows * inv * gain).astype(jnp.bfloat16)

    pl.semaphore_wait(barrier, 27)

    for c in range(CHUNKS):
        for j in range(1, PLANES):
            remote(
                q1.at[c, 0], q1.at[c, j], s1s.at[c], s1r.at[c],
                image_id(lax.rem(z + j, PLANES), p),
            ).start()
    sibling = image_id(z, x * 2 + other)
    w_remote = remote(w_hbm.at[:, other], w_ref.at[core], wsend, wrecv, sibling)

    def scan_images(i, carry):
        doc, end, begin, found = carry
        step = (i >= end).astype(jnp.int32)
        doc = doc + step
        end = end + step * docs_ref[jnp.minimum(doc, PLANES - 1)]
        slot = owner_ref[i]
        begin = jnp.where(slot == me, start_ref[i], begin)
        found = tuple(
            jnp.where(slot == image_id(z, lax.rem(p + d, PEERS)), doc, found[d])
            for d in range(PEERS)
        )
        return doc, end, begin, found

    zero = jnp.int32(0)
    _, _, begin, doc_of = lax.fori_loop(
        0, owner_ref.shape[0], scan_images, (zero, docs_ref[0], zero, (zero,) * PEERS)
    )

    def stage2(c):
        remote(q1.at[c, pl.ds(1, 7)], q1.at[c, pl.ds(1, 7)], s1s.at[c], s1r.at[c], me).wait_recv()
        planes = [q1[c, j] for j in range(PLANES)]
        docs = [lax.rem(z - j + PLANES, PLANES) for j in range(PLANES)]
        for d in range(PEERS):
            rows = planes[0]
            for j in range(1, PLANES):
                rows = jnp.where(doc_of[d] == docs[j], planes[j], rows)
            if d == 0:
                q2[c, 0] = rows
            else:
                sel[c, d] = rows
                remote(
                    sel.at[c, d], q2.at[c, d], s2s.at[c], s2r.at[c],
                    image_id(z, lax.rem(p + d, PEERS)),
                ).start()

    def attention(c):
        lanes = pl.ds(pl.multiple_of((c // 2) * HD, HD), HD)
        remote(q2.at[c, pl.ds(1, 7)], q2.at[c, pl.ds(1, 7)], s2s.at[c], s2r.at[c], me).wait_recv()
        rows = q2[c].reshape(PEERS * ROWS, WIDE)
        rows = jnp.concatenate([rows[:, r * HD : (r + 1) * HD] for r in range(HEADS)], axis=0)
        s = lax.dot_general(k_ref[0:BODY, lanes], rows, NT, preferred_element_type=jnp.float32)
        st = lax.dot_general(kt_ref[c // 2], rows, NT, preferred_element_type=jnp.float32)
        token = lax.broadcasted_iota(jnp.int32, st.shape, 0)
        st = jnp.where(token < TOK - BODY, st, NONE)
        peak = jnp.maximum(jnp.max(s, axis=0, keepdims=True), jnp.max(st, axis=0, keepdims=True))
        w = jnp.exp2(s - peak)
        wt = jnp.exp2(st - peak)
        acc = jnp.dot(
            vt_ref[c // 2, :, 0:BODY], w.astype(jnp.bfloat16), preferred_element_type=jnp.float32
        ) + jnp.dot(
            vt_ref[c // 2, :, BODY : BODY + 128], wt.astype(jnp.bfloat16),
            preferred_element_type=jnp.float32,
        )
        total = jnp.sum(w, axis=0, keepdims=True) + jnp.sum(wt, axis=0, keepdims=True)
        acc = acc * (1.0 / total)
        lse = peak + jnp.log2(total)
        place = lax.rem(lax.broadcasted_iota(jnp.int32, lse.shape, 1), HD)
        position = lax.rem(p - place // ROWS + PEERS, PEERS) * ROWS + lax.rem(place, ROWS)
        lse = jnp.where(position >= begin, lse, NONE)
        high = lse.astype(jnp.bfloat16).astype(jnp.float32)
        middle = (lse - high).astype(jnp.bfloat16).astype(jnp.float32)
        low = lse - high - middle
        stats = [
            piece[:, r * HD : (r + 1) * HD] for piece in (high, middle, low) for r in range(HEADS)
        ]
        stats = jnp.concatenate(stats + [jnp.zeros((128 - len(stats), 128), jnp.float32)], axis=0)
        cols = [acc[:, r * HD : (r + 1) * HD] for r in range(HEADS)] + [stats]
        for r, col in enumerate(cols):
            rows = col.T.astype(jnp.bfloat16).reshape(PEERS, ROWS, HD)
            obuf[c, :, :, r * HD : (r + 1) * HD] = rows
            m3[c, 0, :, r * HD : (r + 1) * HD] = rows[0]
        for d in range(1, PEERS):
            remote(
                obuf.at[c, d], m3.at[c, d], s3s.at[c], s3r.at[c],
                image_id(z, lax.rem(p - d + PEERS, PEERS)),
            ).start()

    def read_block(block):
        stats = block[:, WIDE:].astype(jnp.float32)
        lse = stats[:, 0:HEADS] + stats[:, HEADS : 2 * HEADS] + stats[:, 2 * HEADS : 3 * HEADS]
        return block[:, :WIDE].astype(jnp.float32), lse

    def spread(weight):
        return jnp.concatenate(
            [jnp.broadcast_to(weight[:, r : r + 1], (ROWS, HD)) for r in range(HEADS)], axis=1
        )

    def combine(lses, member):
        top = functools.reduce(
            jnp.maximum, [jnp.where(member[d], lses[d], NONE) for d in range(len(lses))]
        )
        weights = [
            jnp.where(jnp.logical_and(member[d], lses[d] > SEEN), jnp.exp2(lses[d] - top), 0.0)
            for d in range(len(lses))
        ]
        total = functools.reduce(jnp.add, weights)
        some = total > 0.0
        safe = jnp.where(some, total, 1.0)
        return [wt / safe for wt in weights], jnp.where(some, top + jnp.log2(safe), NONE)

    def stage4(c):
        remote(m3.at[c, pl.ds(1, 7)], m3.at[c, pl.ds(1, 7)], s3s.at[c], s3r.at[c], me).wait_recv()
        blocks, lses = zip(*[read_block(m3[c, d]) for d in range(PEERS)])
        factor = [0.0] * PEERS
        found = []
        for j in range(PLANES):
            doc = lax.rem(z + j, PLANES)
            member = [doc_of[d] == doc for d in range(PEERS)]
            weights, lse = combine(lses, member)
            factor = [factor[d] + weights[d] for d in range(PEERS)]
            found.append((member, lse))
        scaled = [blocks[d] * spread(factor[d]) for d in range(PEERS)]
        for j, (member, lse) in enumerate(found):
            rows = functools.reduce(
                jnp.add, [jnp.where(member[d], scaled[d], 0.0) for d in range(PEERS)]
            )
            high = lse.astype(jnp.bfloat16).astype(jnp.float32)
            middle = (lse - high).astype(jnp.bfloat16).astype(jnp.float32)
            low = lse - high - middle
            stats = jnp.concatenate(
                [high, middle, low, jnp.zeros((ROWS, 128 - 3 * HEADS), jnp.float32)], axis=1
            )
            rows = jnp.concatenate([rows, stats], axis=1).astype(jnp.bfloat16)
            if j == 0:
                m4[c, 0] = rows
            else:
                dbuf[c, j] = rows
                remote(
                    dbuf.at[c, j], m4.at[c, j], s4s.at[c], s4r.at[c],
                    image_id(lax.rem(z + j, PLANES), p),
                ).start()

    def stage5(c):
        remote(m4.at[c, pl.ds(1, 7)], m4.at[c, pl.ds(1, 7)], s4s.at[c], s4r.at[c], me).wait_recv()
        blocks, lses = zip(*[read_block(m4[c, j]) for j in range(PLANES)])
        weights, _ = combine(lses, [True] * PLANES)
        rows = functools.reduce(
            jnp.add, [blocks[j] * spread(weights[j]) for j in range(PLANES)]
        ).astype(jnp.bfloat16)
        att[c, 0] = rows[:, : WIDE // 2]
        att[c, 1] = rows[:, WIDE // 2 :]
        ag[c, z, x, core] = att[c, core]
        mine = ag.at[c, z, x, core]
        for j in range(1, PLANES):
            zz = lax.rem(z + j, PLANES)
            remote(att.at[c, core], mine, s5s.at[c], s5r.at[c], image_id(zz, p)).start()
        for j in range(PLANES):
            zz = lax.rem(z + j, PLANES)
            remote(
                att.at[c, other], mine, s5cs.at[c], s5cr.at[c], image_id(zz, x * 2 + other)
            ).start()

    def stage6(c):
        seven, eight = ag.at[c, pl.ds(0, 7), 0, 0], ag.at[c, :, 0, 0]
        remote(seven, seven, s5s.at[c], s5r.at[c], me).wait_recv()
        remote(eight, eight, s5cs.at[c], s5cr.at[c], me).wait_recv()
        for j in range(1, 4):
            remote(
                ag.at[c, :, x], ag.at[c, :, x], s6s.at[c], s6r.at[c],
                image_id(z, lax.rem(x + j, 4) * 2 + core),
            ).start()

    def project(c):
        three = ag.at[c, :, pl.ds(0, 3)]
        remote(three, three, s6s.at[c], s6r.at[c], me).wait_recv()
        w = jnp.concatenate([w_ref[0, c], w_ref[1, c]], axis=1)
        rows = ag[c].reshape(PLANES * PEERS * ROWS, WIDE // 2)
        part[...] += jnp.dot(rows, w, preferred_element_type=jnp.float32)

    stage2(0)
    part[...] = jnp.zeros_like(part)
    w_remote.start()
    v_copy.wait()

    def turn(i, unused):
        body = pl.ds(pl.multiple_of(i * 1280, 1280), 1280)
        for g in range(2):
            vt_ref[g, :, body] = v_ref[body, g * HD : (g + 1) * HD].T
        return unused

    lax.fori_loop(0, BODY // 1280, turn, 0)
    k_copy.wait()
    pad = jnp.zeros((128 - (TOK - BODY), HD), jnp.bfloat16)
    for g in range(2):
        lanes = slice(g * HD, (g + 1) * HD)
        vt_ref[g, :, BODY : BODY + 128] = jnp.concatenate([v_ref[BODY:TOK, lanes], pad], axis=0).T
        kt_ref[g] = jnp.concatenate([k_ref[BODY:TOK, lanes], pad], axis=0)
    w_copy.wait()
    w_remote.wait()

    def turn_of(t, unused):
        def when(lag, stage):
            @pl.when(jnp.logical_and(t >= lag, t < CHUNKS + lag))
            def _():
                stage(t - lag)

        when(-1, stage2)
        when(0, attention)
        when(1, stage4)
        when(2, stage5)
        when(3, stage6)
        when(4, project)
        return unused

    lax.fori_loop(0, CHUNKS + 4, turn_of, 0)

    for j in range(4):
        yy = lax.rem(y + j, 4)
        rows = part[pl.ds(pl.multiple_of(yy * 256, 256), 256), :].astype(jnp.bfloat16)
        for c2 in range(2):
            partb[yy, c2] = rows[:, c2 * 128 : (c2 + 1) * 128]
        if j:
            remote(partb.at[yy, core], rs.at[2 * j], s7s, s7r, me, yy).start()
        remote(partb.at[yy, other], rs.at[2 * j + 1], s7s, s7r, sibling, yy).start()
    seven = rs.at[pl.ds(1, 7)]
    remote(seven, seven, s7s, s7r, me).wait()
    total = partb[y, core].astype(jnp.float32)
    for j in range(1, 8):
        total += rs[j].astype(jnp.float32)
    gate = jnp.tanh(jnp.full((8, 128), gate_ref[0], jnp.float32))[0:1]
    out_ref[...] = (gate * total).astype(jnp.bfloat16)

    for c in range(CHUNKS):
        for buf, sems in ((q1, s1s), (sel, s2s), (obuf, s3s), (dbuf, s4s)):
            seven = buf.at[c, pl.ds(1, 7)]
            remote(seven, seven, sems.at[c], s1r.at[c], me).wait_send()
        seven, eight = ag.at[c, pl.ds(0, 7), 0, 0], ag.at[c, :, 0, 0]
        remote(seven, seven, s5s.at[c], s5r.at[c], me).wait_send()
        remote(eight, eight, s5cs.at[c], s5cr.at[c], me).wait_send()
        three = ag.at[c, :, pl.ds(0, 3)]
        remote(three, three, s6s.at[c], s6r.at[c], me).wait_send()


def on_device(
    queries, query_gain, keys, values, out_weight, gate, doc_images, image_owner, image_start
):
    vmem = pl.BlockSpec(memory_space=pltpu.VMEM)
    smem = pl.BlockSpec(memory_space=pltpu.SMEM)
    hbm = pl.BlockSpec(memory_space=pl.ANY)
    bf16, f32 = jnp.bfloat16, jnp.float32
    dma = pltpu.SemaphoreType.DMA
    return pl.pallas_call(
        kernel,
        out_shape=jax.ShapeDtypeStruct((256, 128), bf16),
        in_specs=[vmem, vmem, hbm, hbm, hbm, smem, smem, smem, smem],
        out_specs=vmem,
        scratch_shapes=[
            pltpu.VMEM((TOK, 256), bf16),
            pltpu.VMEM((TOK, 256), bf16),
            pltpu.VMEM((2, HD, BODY + 128), bf16),
            pltpu.VMEM((2, 128, HD), bf16),
            pltpu.VMEM((2, CHUNKS, 256, 128), bf16),
            pltpu.VMEM((CHUNKS, PLANES, ROWS, WIDE), bf16),
            pltpu.VMEM((CHUNKS, PEERS, ROWS, WIDE), bf16),
            pltpu.VMEM((CHUNKS, PEERS, ROWS, WIDE), bf16),
            pltpu.VMEM((CHUNKS, PEERS, ROWS, BLOCK), bf16),
            pltpu.VMEM((CHUNKS, PEERS, ROWS, BLOCK), bf16),
            pltpu.VMEM((CHUNKS, PLANES, ROWS, BLOCK), bf16),
            pltpu.VMEM((CHUNKS, PLANES, ROWS, BLOCK), bf16),
            pltpu.VMEM((CHUNKS, 2, ROWS, WIDE // 2), bf16),
            pltpu.VMEM((CHUNKS, PLANES, 4, 2, ROWS, WIDE // 2), bf16),
            pltpu.VMEM((PLANES * PEERS * ROWS, 256), f32),
            pltpu.VMEM((4, 2, 256, 128), bf16),
            pltpu.VMEM((8, 256, 128), bf16),
            dma(()), dma(()), dma(()), dma(()), dma(()),
        ]
        + [dma((CHUNKS,))] * 14
        + [dma(()), dma(())],
        compiler_params=pltpu.CompilerParams(
            collective_id=0, has_side_effects=True, vmem_limit_bytes=60 << 20
        ),
    )(
        queries, query_gain.reshape(1, HD), keys, values,
        out_weight.reshape(CHUNKS, 2, 256, 128), gate, doc_images, image_owner, image_start,
    )


def solution(mesh):
    placed = (
        P("image", "tensor"),
        P(),
        P("image", None, "tensor"),
        P("image", None, "tensor"),
        P("tensor", "image"),
        P(),
        P(),
        P(),
        P(),
    )
    return jax.shard_map(
        on_device, mesh=mesh, in_specs=placed, out_specs=P("tensor", "image"), check_vma=False
    )
```

```python
import functools
import math

import jax
import jax.numpy as jnp
from jax import lax
from jax.experimental import pallas as pl
from jax.experimental.pallas import tpu as pltpu
from jax.sharding import PartitionSpec as P

HD = 128
ROWS = 16
PLANES = 8
PEERS = 8
CHUNKS = 4
HEADS = 4
WIDE = HEADS * HD
BLOCK = WIDE + 128
TOK = 6404
BODY = 6400
NONE = -1e30
SEEN = -1e29
MESH = pl.DeviceIdType.MESH
NT = (((1,), (1,)), ((), ()))
FAR = (4, 3, 5, 2, 6, 1, 7)


def kernel(
    q_ref, gain_ref, k_hbm, v_hbm, w_hbm, gate_ref, docs_ref, owner_ref, start_ref,
    out_ref,
    k_ref, v_ref, vt_ref, kt_ref, w_ref,
    q1, sel, q2, obuf, m3, dbuf, m4, ag, part, partb, rs,
    ksem, vsem, wsem,
    s1s, s1r, s2s, s2r, s3s, s3r, s4s, s4r, s5s, s5r, ws, wr, wfs, wfr, s7s, s7r,
):
    me = lax.axis_index("image")
    y = lax.axis_index("tensor")
    z, p = me // PEERS, lax.rem(me, PEERS)
    x, core = p // 2, lax.rem(p, 2)
    other = 1 - core

    def image_id(zz, pp):
        return zz * PEERS + pp

    def remote(src, dst, ssem, rsem, img, yy=None):
        return pltpu.make_async_remote_copy(
            src_ref=src, dst_ref=dst, send_sem=ssem, recv_sem=rsem,
            device_id=(img, y if yy is None else yy), device_id_type=MESH,
        )

    k_copy = pltpu.make_async_copy(k_hbm.at[0], k_ref, ksem)
    v_copy = pltpu.make_async_copy(v_hbm.at[0], v_ref, vsem)
    w_copy = pltpu.make_async_copy(w_hbm, w_ref.at[p], wsem)
    v_copy.start()
    k_copy.start()
    w_copy.start()

    barrier = pltpu.get_barrier_semaphore()

    def greet(img, yy):
        pl.semaphore_signal(barrier, inc=1, device_id=(img, yy), device_id_type=MESH)

    for j in range(1, PLANES):
        greet(image_id(lax.rem(z + j, PLANES), p), y)
    for j in range(4):
        for d in range(PEERS):
            if j or d:
                greet(image_id(z, lax.rem(p + d, PEERS)), lax.rem(y + j, 4))

    gain = gain_ref[...].astype(jnp.float32) * (math.log2(math.e) / math.sqrt(HD))
    for h in range(CHUNKS * HEADS):
        rows = q_ref[:, h * HD : (h + 1) * HD].astype(jnp.float32)
        inv = lax.rsqrt(jnp.mean(rows * rows, axis=1, keepdims=True) + 1e-05)
        lo = (h % HEADS) * HD
        q1[h // HEADS, 0, :, lo : lo + HD] = (rows * inv * gain).astype(jnp.bfloat16)

    pl.semaphore_wait(barrier, 38)

    for c in range(CHUNKS):
        for j in FAR:
            remote(
                q1.at[c, 0], q1.at[c, j], s1s.at[c], s1r.at[c],
                image_id(lax.rem(z + j, PLANES), p),
            ).start()
    sibling = image_id(z, x * 2 + other)

    def send_weight(c):
        for d in range(1, PEERS):
            pp = lax.rem(p + d, PEERS)
            half = lax.rem(pp, 2)
            remote(
                w_hbm.at[c, half], w_ref.at[p, c, half], ws.at[c], wr.at[c], image_id(z, pp)
            ).start()

    def pass_weight(c):
        seven = w_ref.at[pl.ds(0, 7), c, core]
        remote(seven, seven, ws.at[c], wr.at[c], me).wait_recv()
        for d in range(2, PEERS, 2):
            block = w_ref.at[lax.rem(p + d, PEERS), c, core]
            remote(block, block, wfs.at[c], wfr.at[c], sibling).start()
        for d in range(2, PEERS, 2):
            block = w_ref.at[lax.rem(x * 2 + other + d, PEERS), c, core]
            remote(block, block, wfs.at[c], wfr.at[c], sibling).start()
        block = w_hbm.at[c, core]
        remote(block, w_ref.at[p, c, core], wfs.at[c], wfr.at[c], sibling).start()

    send_weight(0)

    def scan_images(i, carry):
        doc, end, begin, found = carry
        step = (i >= end).astype(jnp.int32)
        doc = doc + step
        end = end + step * docs_ref[jnp.minimum(doc, PLANES - 1)]
        slot = owner_ref[i]
        begin = jnp.where(slot == me, start_ref[i], begin)
        found = tuple(
            jnp.where(slot == image_id(z, lax.rem(p + d, PEERS)), doc, found[d])
            for d in range(PEERS)
        )
        return doc, end, begin, found

    zero = jnp.int32(0)
    _, _, begin, doc_of = lax.fori_loop(
        0, owner_ref.shape[0], scan_images, (zero, docs_ref[0], zero, (zero,) * PEERS)
    )

    def stage2(c):
        remote(q1.at[c, pl.ds(1, 7)], q1.at[c, pl.ds(1, 7)], s1s.at[c], s1r.at[c], me).wait_recv()
        planes = [q1[c, j] for j in range(PLANES)]
        docs = [lax.rem(z - j + PLANES, PLANES) for j in range(PLANES)]
        for d in FAR + (0,):
            rows = planes[0]
            for j in range(1, PLANES):
                rows = jnp.where(doc_of[d] == docs[j], planes[j], rows)
            if d == 0:
                q2[c, 0] = rows
            else:
                sel[c, d] = rows
                remote(
                    sel.at[c, d], q2.at[c, d], s2s.at[c], s2r.at[c],
                    image_id(z, lax.rem(p + d, PEERS)),
                ).start()

    def attention(c):
        lanes = pl.ds(pl.multiple_of((c // 2) * HD, HD), HD)
        remote(q2.at[c, pl.ds(1, 7)], q2.at[c, pl.ds(1, 7)], s2s.at[c], s2r.at[c], me).wait_recv()
        rows = q2[c].reshape(PEERS * ROWS, WIDE)
        rows = jnp.concatenate([rows[:, r * HD : (r + 1) * HD] for r in range(HEADS)], axis=0)
        s = lax.dot_general(k_ref[0:BODY, lanes], rows, NT, preferred_element_type=jnp.float32)
        st = lax.dot_general(kt_ref[c // 2], rows, NT, preferred_element_type=jnp.float32)
        token = lax.broadcasted_iota(jnp.int32, st.shape, 0)
        st = jnp.where(token < TOK - BODY, st, NONE)
        peak = jnp.maximum(jnp.max(s, axis=0, keepdims=True), jnp.max(st, axis=0, keepdims=True))
        w = jnp.exp2(s - peak)
        wt = jnp.exp2(st - peak)
        acc = jnp.dot(
            vt_ref[c // 2, :, 0:BODY], w.astype(jnp.bfloat16), preferred_element_type=jnp.float32
        ) + jnp.dot(
            vt_ref[c // 2, :, BODY : BODY + 128], wt.astype(jnp.bfloat16),
            preferred_element_type=jnp.float32,
        )
        total = jnp.sum(w, axis=0, keepdims=True) + jnp.sum(wt, axis=0, keepdims=True)
        acc = acc * (1.0 / total)
        lse = peak + jnp.log2(total)
        place = lax.rem(lax.broadcasted_iota(jnp.int32, lse.shape, 1), HD)
        position = lax.rem(p - place // ROWS + PEERS, PEERS) * ROWS + lax.rem(place, ROWS)
        lse = jnp.where(position >= begin, lse, NONE)
        high = lse.astype(jnp.bfloat16).astype(jnp.float32)
        middle = (lse - high).astype(jnp.bfloat16).astype(jnp.float32)
        low = lse - high - middle
        stats = [
            piece[:, r * HD : (r + 1) * HD] for piece in (high, middle, low) for r in range(HEADS)
        ]
        stats = jnp.concatenate(stats + [jnp.zeros((128 - len(stats), 128), jnp.float32)], axis=0)
        cols = [acc[:, r * HD : (r + 1) * HD] for r in range(HEADS)] + [stats]
        for r, col in enumerate(cols):
            rows = col.T.astype(jnp.bfloat16).reshape(PEERS, ROWS, HD)
            obuf[c, :, :, r * HD : (r + 1) * HD] = rows
            m3[c, 0, :, r * HD : (r + 1) * HD] = rows[0]
        for d in FAR:
            remote(
                obuf.at[c, d], m3.at[c, d], s3s.at[c], s3r.at[c],
                image_id(z, lax.rem(p - d + PEERS, PEERS)),
            ).start()

    def read_block(block):
        stats = block[:, WIDE:].astype(jnp.float32)
        lse = stats[:, 0:HEADS] + stats[:, HEADS : 2 * HEADS] + stats[:, 2 * HEADS : 3 * HEADS]
        return block[:, :WIDE].astype(jnp.float32), lse

    def spread(weight):
        return jnp.concatenate(
            [jnp.broadcast_to(weight[:, r : r + 1], (ROWS, HD)) for r in range(HEADS)], axis=1
        )

    def combine(lses, member):
        top = functools.reduce(
            jnp.maximum, [jnp.where(member[d], lses[d], NONE) for d in range(len(lses))]
        )
        weights = [
            jnp.where(jnp.logical_and(member[d], lses[d] > SEEN), jnp.exp2(lses[d] - top), 0.0)
            for d in range(len(lses))
        ]
        total = functools.reduce(jnp.add, weights)
        some = total > 0.0
        safe = jnp.where(some, total, 1.0)
        return [wt / safe for wt in weights], jnp.where(some, top + jnp.log2(safe), NONE)

    def stage4(c):
        remote(m3.at[c, pl.ds(1, 7)], m3.at[c, pl.ds(1, 7)], s3s.at[c], s3r.at[c], me).wait_recv()
        blocks, lses = zip(*[read_block(m3[c, d]) for d in range(PEERS)])
        factor = [0.0] * PEERS
        found = []
        for j in range(PLANES):
            doc = lax.rem(z + j, PLANES)
            member = [doc_of[d] == doc for d in range(PEERS)]
            weights, lse = combine(lses, member)
            factor = [factor[d] + weights[d] for d in range(PEERS)]
            found.append((member, lse))
        scaled = [blocks[d] * spread(factor[d]) for d in range(PEERS)]
        for j in FAR + (0,):
            member, lse = found[j]
            rows = functools.reduce(
                jnp.add, [jnp.where(member[d], scaled[d], 0.0) for d in range(PEERS)]
            )
            high = lse.astype(jnp.bfloat16).astype(jnp.float32)
            middle = (lse - high).astype(jnp.bfloat16).astype(jnp.float32)
            low = lse - high - middle
            stats = jnp.concatenate(
                [high, middle, low, jnp.zeros((ROWS, 128 - 3 * HEADS), jnp.float32)], axis=1
            )
            rows = jnp.concatenate([rows, stats], axis=1).astype(jnp.bfloat16)
            if j == 0:
                m4[c, 0] = rows
            else:
                dbuf[c, j] = rows
                remote(
                    dbuf.at[c, j], m4.at[c, j], s4s.at[c], s4r.at[c],
                    image_id(lax.rem(z + j, PLANES), p),
                ).start()

    def stage5(c):
        remote(m4.at[c, pl.ds(1, 7)], m4.at[c, pl.ds(1, 7)], s4s.at[c], s4r.at[c], me).wait_recv()
        blocks, lses = zip(*[read_block(m4[c, j]) for j in range(PLANES)])
        weights, _ = combine(lses, [True] * PLANES)
        rows = functools.reduce(
            jnp.add, [blocks[j] * spread(weights[j]) for j in range(PLANES)]
        ).astype(jnp.bfloat16)
        ag[c, 0] = rows
        for j in FAR:
            remote(
                ag.at[c, 0], ag.at[c, j], s5s.at[c], s5r.at[c],
                image_id(lax.rem(z + j, PLANES), p),
            ).start()

    def project(c):
        seven = ag.at[c, pl.ds(1, 7)]
        remote(seven, seven, s5s.at[c], s5r.at[c], me).wait_recv()
        seven = w_ref.at[pl.ds(0, 7), c, other]
        remote(seven, seven, wfs.at[c], wfr.at[c], me).wait_recv()
        rows = ag[c].reshape(PLANES * ROWS, WIDE)
        for d in range(PEERS):
            cols = slice(d * 128, (d + 1) * 128)
            part[:, cols] += jnp.dot(
                rows, w_ref[d, c].reshape(WIDE, 128), preferred_element_type=jnp.float32
            )

    stage2(0)
    part[...] = jnp.zeros_like(part)
    v_copy.wait()

    def turn(i, unused):
        body = pl.ds(pl.multiple_of(i * 1280, 1280), 1280)
        for g in range(2):
            vt_ref[g, :, body] = v_ref[body, g * HD : (g + 1) * HD].T
        return unused

    lax.fori_loop(0, BODY // 1280, turn, 0)
    k_copy.wait()
    pad = jnp.zeros((128 - (TOK - BODY), HD), jnp.bfloat16)
    for g in range(2):
        lanes = slice(g * HD, (g + 1) * HD)
        vt_ref[g, :, BODY : BODY + 128] = jnp.concatenate([v_ref[BODY:TOK, lanes], pad], axis=0).T
        kt_ref[g] = jnp.concatenate([k_ref[BODY:TOK, lanes], pad], axis=0)
    w_copy.wait()

    def turn_of(t, unused):
        def when(lag, stage):
            @pl.when(jnp.logical_and(t >= lag, t < CHUNKS + lag))
            def _():
                stage(t - lag)

        when(-1, stage2)
        when(-1, send_weight)
        when(0, attention)
        when(1, stage4)
        when(2, stage5)
        when(1, pass_weight)
        when(3, project)
        return unused

    lax.fori_loop(0, CHUNKS + 3, turn_of, 0)

    for j in range(4):
        yy = lax.rem(y + j, 4)
        for e in range(2):
            slot = lax.rem(z - (2 * yy + e) + PLANES, PLANES)
            rows = part[pl.ds(pl.multiple_of(slot * ROWS, ROWS), ROWS), :].astype(jnp.bfloat16)
            for d in range(PEERS):
                partb[j, d, e] = rows[:, d * 128 : (d + 1) * 128]
        for d in range(PEERS):
            if j or d:
                pp = lax.rem(p + d, PEERS)
                remote(partb.at[j, pp], rs.at[8 * j + d], s7s, s7r, image_id(z, pp), yy).start()
    most = rs.at[pl.ds(1, 31)]
    remote(most, most, s7s, s7r, me).wait()
    gate = jnp.tanh(jnp.full((8, 128), gate_ref[0], jnp.float32))[0:1]
    rs[0] = partb[0, p]
    for d in range(PEERS):
        total = rs[d].astype(jnp.float32)
        for j in range(1, 4):
            total += rs[8 * j + d].astype(jnp.float32)
        out_ref[:, lax.rem(p - d + PEERS, PEERS)] = (gate * total).astype(jnp.bfloat16)

    for c in range(CHUNKS):
        for buf, sems in ((q1, s1s), (sel, s2s), (obuf, s3s), (dbuf, s4s), (ag, s5s)):
            seven = buf.at[c, pl.ds(1, 7)]
            remote(seven, seven, sems.at[c], s1r.at[c], me).wait_send()
        seven = w_ref.at[pl.ds(0, 7), c, 0]
        remote(seven, seven, ws.at[c], wr.at[c], me).wait_send()
        remote(seven, seven, wfs.at[c], wfr.at[c], me).wait_send()


def on_device(
    queries, query_gain, keys, values, out_weight, gate, doc_images, image_owner, image_start
):
    vmem = pl.BlockSpec(memory_space=pltpu.VMEM)
    smem = pl.BlockSpec(memory_space=pltpu.SMEM)
    hbm = pl.BlockSpec(memory_space=pl.ANY)
    bf16, f32 = jnp.bfloat16, jnp.float32
    dma = pltpu.SemaphoreType.DMA
    out = pl.pallas_call(
        kernel,
        out_shape=jax.ShapeDtypeStruct((2, PEERS, ROWS, 128), bf16),
        in_specs=[vmem, vmem, hbm, hbm, hbm, smem, smem, smem, smem],
        out_specs=vmem,
        scratch_shapes=[
            pltpu.VMEM((TOK, 256), bf16),
            pltpu.VMEM((TOK, 256), bf16),
            pltpu.VMEM((2, HD, BODY + 128), bf16),
            pltpu.VMEM((2, 128, HD), bf16),
            pltpu.VMEM((PEERS, CHUNKS, 2, 256, 128), bf16),
            pltpu.VMEM((CHUNKS, PLANES, ROWS, WIDE), bf16),
            pltpu.VMEM((CHUNKS, PEERS, ROWS, WIDE), bf16),
            pltpu.VMEM((CHUNKS, PEERS, ROWS, WIDE), bf16),
            pltpu.VMEM((CHUNKS, PEERS, ROWS, BLOCK), bf16),
            pltpu.VMEM((CHUNKS, PEERS, ROWS, BLOCK), bf16),
            pltpu.VMEM((CHUNKS, PLANES, ROWS, BLOCK), bf16),
            pltpu.VMEM((CHUNKS, PLANES, ROWS, BLOCK), bf16),
            pltpu.VMEM((CHUNKS, PLANES, ROWS, WIDE), bf16),
            pltpu.VMEM((PLANES * ROWS, PEERS * 128), f32),
            pltpu.VMEM((4, PEERS, 2, ROWS, 128), bf16),
            pltpu.VMEM((4 * PEERS, 2, ROWS, 128), bf16),
            dma(()), dma(()), dma(()),
        ]
        + [dma((CHUNKS,))] * 14
        + [dma(()), dma(())],
        compiler_params=pltpu.CompilerParams(
            collective_id=0, has_side_effects=True, vmem_limit_bytes=60 << 20
        ),
    )(
        queries, query_gain.reshape(1, HD), keys, values,
        out_weight.reshape(CHUNKS, 2, 256, 128), gate, doc_images, image_owner, image_start,
    )
    return out.reshape(256, 128)


def solution(mesh):
    placed = (
        P("image", "tensor"),
        P(),
        P("image", None, "tensor"),
        P("image", None, "tensor"),
        P("tensor", "image"),
        P(),
        P(),
        P(),
        P(),
    )
    return jax.shard_map(
        on_device, mesh=mesh, in_specs=placed, out_specs=P("tensor", "image"), check_vma=False
    )
```

```python
import functools
import math

import jax
import jax.numpy as jnp
from jax import lax
from jax.experimental import pallas as pl
from jax.experimental.pallas import tpu as pltpu
from jax.sharding import PartitionSpec as P

HD = 128
ROWS = 16
PLANES = 8
PEERS = 8
CHUNKS = 4
HEADS = 4
WIDE = HEADS * HD
BLOCK = WIDE + 128
TOK = 6404
BODY = 6400
NONE = -1e30
SEEN = -1e29
MESH = pl.DeviceIdType.MESH
NT = (((1,), (1,)), ((), ()))
FAR = (4, 3, 5, 2, 6, 1, 7)


def kernel(
    q_ref, gain_ref, k_hbm, v_hbm, w_hbm, gate_ref, docs_ref, owner_ref, start_ref,
    out_ref,
    k_ref, v_ref, vt_ref, kt_ref, w_ref,
    q1, sel, q2, obuf, m3, dbuf, m4, ag, part, partb, rs,
    ksem, vsem, wsem,
    s1s, s1r, s2s, s2r, s3s, s3r, s4s, s4r, s5s, s5r, ws, wr, wfs, wfr, s7s, s7r,
):
    me = lax.axis_index("image")
    y = lax.axis_index("tensor")
    z, p = me // PEERS, lax.rem(me, PEERS)
    x, core = p // 2, lax.rem(p, 2)
    other = 1 - core

    def image_id(zz, pp):
        return zz * PEERS + pp

    def remote(src, dst, ssem, rsem, img, yy=None):
        return pltpu.make_async_remote_copy(
            src_ref=src, dst_ref=dst, send_sem=ssem, recv_sem=rsem,
            device_id=(img, y if yy is None else yy), device_id_type=MESH,
        )

    k_copy = pltpu.make_async_copy(k_hbm.at[0], k_ref, ksem)
    v_copy = pltpu.make_async_copy(v_hbm.at[0], v_ref, vsem)
    w_copy = pltpu.make_async_copy(w_hbm, w_ref.at[p], wsem)
    v_copy.start()
    k_copy.start()
    w_copy.start()

    barrier = pltpu.get_barrier_semaphore()

    def greet(img, yy):
        pl.semaphore_signal(barrier, inc=1, device_id=(img, yy), device_id_type=MESH)

    for j in range(1, PLANES):
        greet(image_id(lax.rem(z + j, PLANES), p), y)
    for j in range(4):
        for d in range(PEERS):
            if j or d:
                greet(image_id(z, lax.rem(p + d, PEERS)), lax.rem(y + j, 4))

    gain = gain_ref[...].astype(jnp.float32) * (math.log2(math.e) / math.sqrt(HD))
    for h in range(CHUNKS * HEADS):
        rows = q_ref[:, h * HD : (h + 1) * HD].astype(jnp.float32)
        inv = lax.rsqrt(jnp.mean(rows * rows, axis=1, keepdims=True) + 1e-05)
        lo = (h % HEADS) * HD
        q1[h // HEADS, 0, :, lo : lo + HD] = (rows * inv * gain).astype(jnp.bfloat16)

    pl.semaphore_wait(barrier, 38)

    for c in range(CHUNKS):
        for j in FAR:
            remote(
                q1.at[c, 0], q1.at[c, j], s1s.at[c], s1r.at[c],
                image_id(lax.rem(z + j, PLANES), p),
            ).start()
    sibling = image_id(z, x * 2 + other)

    def send_weight(c, steps):
        for step in steps:
            for e in range(2):
                pp = lax.rem(x + step, 4) * 2 + e
                remote(
                    w_hbm.at[c, e], w_ref.at[p, c, e], ws.at[c], wr.at[c], image_id(z, pp)
                ).start()

    def near_weight(c):
        remote(
            w_hbm.at[c, other], w_ref.at[p, c, other], ws.at[c], wr.at[c], sibling
        ).start()
        send_weight(c, (1, 3))

    def far_weight(c):
        send_weight(c, (2,))

    def pass_weight(c):
        seven = w_ref.at[pl.ds(0, 7), c, core]
        remote(seven, seven, ws.at[c], wr.at[c], me).wait_recv()
        for d in range(2, PEERS, 2):
            block = w_ref.at[lax.rem(p + d, PEERS), c, core]
            remote(block, block, wfs.at[c], wfr.at[c], sibling).start()
        for d in range(2, PEERS, 2):
            block = w_ref.at[lax.rem(x * 2 + other + d, PEERS), c, core]
            remote(block, block, wfs.at[c], wfr.at[c], sibling).start()
        block = w_hbm.at[c, core]
        remote(block, w_ref.at[p, c, core], wfs.at[c], wfr.at[c], sibling).start()

    near_weight(0)
    far_weight(0)

    def scan_images(i, carry):
        doc, end, begin, found = carry
        step = (i >= end).astype(jnp.int32)
        doc = doc + step
        end = end + step * docs_ref[jnp.minimum(doc, PLANES - 1)]
        slot = owner_ref[i]
        begin = jnp.where(slot == me, start_ref[i], begin)
        found = tuple(
            jnp.where(slot == image_id(z, lax.rem(p + d, PEERS)), doc, found[d])
            for d in range(PEERS)
        )
        return doc, end, begin, found

    zero = jnp.int32(0)
    _, _, begin, doc_of = lax.fori_loop(
        0, owner_ref.shape[0], scan_images, (zero, docs_ref[0], zero, (zero,) * PEERS)
    )

    def stage2(c):
        remote(q1.at[c, pl.ds(1, 7)], q1.at[c, pl.ds(1, 7)], s1s.at[c], s1r.at[c], me).wait_recv()
        planes = [q1[c, j] for j in range(PLANES)]
        docs = [lax.rem(z - j + PLANES, PLANES) for j in range(PLANES)]
        for d in FAR + (0,):
            rows = planes[0]
            for j in range(1, PLANES):
                rows = jnp.where(doc_of[d] == docs[j], planes[j], rows)
            if d == 0:
                q2[c, 0] = rows
            else:
                sel[c, d] = rows
                remote(
                    sel.at[c, d], q2.at[c, d], s2s.at[c], s2r.at[c],
                    image_id(z, lax.rem(p + d, PEERS)),
                ).start()

    def attention(c):
        lanes = pl.ds(pl.multiple_of((c // 2) * HD, HD), HD)
        remote(q2.at[c, pl.ds(1, 7)], q2.at[c, pl.ds(1, 7)], s2s.at[c], s2r.at[c], me).wait_recv()
        rows = q2[c].reshape(PEERS * ROWS, WIDE)
        rows = jnp.concatenate([rows[:, r * HD : (r + 1) * HD] for r in range(HEADS)], axis=0)
        s = lax.dot_general(k_ref[0:BODY, lanes], rows, NT, preferred_element_type=jnp.float32)
        st = lax.dot_general(kt_ref[c // 2], rows, NT, preferred_element_type=jnp.float32)
        token = lax.broadcasted_iota(jnp.int32, st.shape, 0)
        st = jnp.where(token < TOK - BODY, st, NONE)
        peak = jnp.maximum(jnp.max(s, axis=0, keepdims=True), jnp.max(st, axis=0, keepdims=True))
        w = jnp.exp2(s - peak)
        wt = jnp.exp2(st - peak)
        acc = jnp.dot(
            vt_ref[c // 2, :, 0:BODY], w.astype(jnp.bfloat16), preferred_element_type=jnp.float32
        ) + jnp.dot(
            vt_ref[c // 2, :, BODY : BODY + 128], wt.astype(jnp.bfloat16),
            preferred_element_type=jnp.float32,
        )
        total = jnp.sum(w, axis=0, keepdims=True) + jnp.sum(wt, axis=0, keepdims=True)
        acc = acc * (1.0 / total)
        lse = peak + jnp.log2(total)
        place = lax.rem(lax.broadcasted_iota(jnp.int32, lse.shape, 1), HD)
        position = lax.rem(p - place // ROWS + PEERS, PEERS) * ROWS + lax.rem(place, ROWS)
        lse = jnp.where(position >= begin, lse, NONE)
        high = lse.astype(jnp.bfloat16).astype(jnp.float32)
        middle = (lse - high).astype(jnp.bfloat16).astype(jnp.float32)
        low = lse - high - middle
        stats = [
            piece[:, r * HD : (r + 1) * HD] for piece in (high, middle, low) for r in range(HEADS)
        ]
        stats = jnp.concatenate(stats + [jnp.zeros((128 - len(stats), 128), jnp.float32)], axis=0)
        cols = [acc[:, r * HD : (r + 1) * HD] for r in range(HEADS)] + [stats]
        for r, col in enumerate(cols):
            rows = col.T.astype(jnp.bfloat16).reshape(PEERS, ROWS, HD)
            obuf[c, :, :, r * HD : (r + 1) * HD] = rows
            m3[c, 0, :, r * HD : (r + 1) * HD] = rows[0]
        for d in FAR:
            remote(
                obuf.at[c, d], m3.at[c, d], s3s.at[c], s3r.at[c],
                image_id(z, lax.rem(p - d + PEERS, PEERS)),
            ).start()

    def read_block(block):
        stats = block[:, WIDE:].astype(jnp.float32)
        lse = stats[:, 0:HEADS] + stats[:, HEADS : 2 * HEADS] + stats[:, 2 * HEADS : 3 * HEADS]
        return block[:, :WIDE].astype(jnp.float32), lse

    def spread(weight):
        return jnp.concatenate(
            [jnp.broadcast_to(weight[:, r : r + 1], (ROWS, HD)) for r in range(HEADS)], axis=1
        )

    def combine(lses, member):
        top = functools.reduce(
            jnp.maximum, [jnp.where(member[d], lses[d], NONE) for d in range(len(lses))]
        )
        weights = [
            jnp.where(jnp.logical_and(member[d], lses[d] > SEEN), jnp.exp2(lses[d] - top), 0.0)
            for d in range(len(lses))
        ]
        total = functools.reduce(jnp.add, weights)
        some = total > 0.0
        safe = jnp.where(some, total, 1.0)
        return [wt / safe for wt in weights], jnp.where(some, top + jnp.log2(safe), NONE)

    def stage4(c):
        remote(m3.at[c, pl.ds(1, 7)], m3.at[c, pl.ds(1, 7)], s3s.at[c], s3r.at[c], me).wait_recv()
        blocks, lses = zip(*[read_block(m3[c, d]) for d in range(PEERS)])
        factor = [0.0] * PEERS
        found = []
        for j in range(PLANES):
            doc = lax.rem(z + j, PLANES)
            member = [doc_of[d] == doc for d in range(PEERS)]
            weights, lse = combine(lses, member)
            factor = [factor[d] + weights[d] for d in range(PEERS)]
            found.append((member, lse))
        scaled = [blocks[d] * spread(factor[d]) for d in range(PEERS)]
        for j in FAR + (0,):
            member, lse = found[j]
            rows = functools.reduce(
                jnp.add, [jnp.where(member[d], scaled[d], 0.0) for d in range(PEERS)]
            )
            high = lse.astype(jnp.bfloat16).astype(jnp.float32)
            middle = (lse - high).astype(jnp.bfloat16).astype(jnp.float32)
            low = lse - high - middle
            stats = jnp.concatenate(
                [high, middle, low, jnp.zeros((ROWS, 128 - 3 * HEADS), jnp.float32)], axis=1
            )
            rows = jnp.concatenate([rows, stats], axis=1).astype(jnp.bfloat16)
            if j == 0:
                m4[c, 0] = rows
            else:
                dbuf[c, j] = rows
                remote(
                    dbuf.at[c, j], m4.at[c, j], s4s.at[c], s4r.at[c],
                    image_id(lax.rem(z + j, PLANES), p),
                ).start()

    def stage5(c):
        remote(m4.at[c, pl.ds(1, 7)], m4.at[c, pl.ds(1, 7)], s4s.at[c], s4r.at[c], me).wait_recv()
        blocks, lses = zip(*[read_block(m4[c, j]) for j in range(PLANES)])
        weights, _ = combine(lses, [True] * PLANES)
        rows = functools.reduce(
            jnp.add, [blocks[j] * spread(weights[j]) for j in range(PLANES)]
        ).astype(jnp.bfloat16)
        ag[c, 0] = rows
        for j in FAR:
            remote(
                ag.at[c, 0], ag.at[c, j], s5s.at[c], s5r.at[c],
                image_id(lax.rem(z + j, PLANES), p),
            ).start()

    def project(c):
        seven = ag.at[c, pl.ds(1, 7)]
        remote(seven, seven, s5s.at[c], s5r.at[c], me).wait_recv()
        seven = w_ref.at[pl.ds(0, 7), c, other]
        remote(seven, seven, wfs.at[c], wfr.at[c], me).wait_recv()
        rows = ag[c].reshape(PLANES * ROWS, WIDE)
        for d in range(PEERS):
            cols = slice(d * 128, (d + 1) * 128)
            part[:, cols] += jnp.dot(
                rows, w_ref[d, c].reshape(WIDE, 128), preferred_element_type=jnp.float32
            )

    stage2(0)
    part[...] = jnp.zeros_like(part)
    v_copy.wait()

    def turn(i, unused):
        body = pl.ds(pl.multiple_of(i * 1280, 1280), 1280)
        for g in range(2):
            vt_ref[g, :, body] = v_ref[body, g * HD : (g + 1) * HD].T
        return unused

    lax.fori_loop(0, BODY // 1280, turn, 0)
    k_copy.wait()
    pad = jnp.zeros((128 - (TOK - BODY), HD), jnp.bfloat16)
    for g in range(2):
        lanes = slice(g * HD, (g + 1) * HD)
        vt_ref[g, :, BODY : BODY + 128] = jnp.concatenate([v_ref[BODY:TOK, lanes], pad], axis=0).T
        kt_ref[g] = jnp.concatenate([k_ref[BODY:TOK, lanes], pad], axis=0)
    w_copy.wait()

    def turn_of(t, unused):
        def at(first, last, stage, *args):
            @pl.when(jnp.logical_and(t >= first, t <= last))
            def _():
                stage(*args)

        at(0, 2, stage2, t + 1)
        at(0, 0, near_weight, 1)
        at(1, 1, far_weight, 1)
        at(2, 2, near_weight, 2)
        at(0, 3, attention, t)
        at(3, 3, far_weight, 2)
        at(3, 3, near_weight, 3)
        at(3, 3, far_weight, 3)
        at(1, 3, stage4, t - 1)
        at(2, 3, stage5, t - 2)
        at(2, 2, pass_weight, t - 2)
        return unused

    lax.fori_loop(0, CHUNKS, turn_of, 0)
    stage4(3)
    pass_weight(1)
    stage5(2)
    project(0)
    pass_weight(2)
    project(1)
    stage5(3)
    pass_weight(3)
    project(2)
    project(3)

    for j in range(4):
        yy = lax.rem(y + j, 4)
        for e in range(2):
            slot = lax.rem(z - (2 * yy + e) + PLANES, PLANES)
            rows = part[pl.ds(pl.multiple_of(slot * ROWS, ROWS), ROWS), :].astype(jnp.bfloat16)
            for d in range(PEERS):
                partb[j, d, e] = rows[:, d * 128 : (d + 1) * 128]
        for d in range(PEERS):
            if j or d:
                pp = lax.rem(p + d, PEERS)
                remote(partb.at[j, pp], rs.at[8 * j + d], s7s, s7r, image_id(z, pp), yy).start()
    most = rs.at[pl.ds(1, 31)]
    remote(most, most, s7s, s7r, me).wait()
    gate = jnp.tanh(jnp.full((8, 128), gate_ref[0], jnp.float32))[0:1]
    rs[0] = partb[0, p]
    for d in range(PEERS):
        total = rs[d].astype(jnp.float32)
        for j in range(1, 4):
            total += rs[8 * j + d].astype(jnp.float32)
        out_ref[:, lax.rem(p - d + PEERS, PEERS)] = (gate * total).astype(jnp.bfloat16)

    for c in range(CHUNKS):
        for buf, sems in ((q1, s1s), (sel, s2s), (obuf, s3s), (dbuf, s4s), (ag, s5s)):
            seven = buf.at[c, pl.ds(1, 7)]
            remote(seven, seven, sems.at[c], s1r.at[c], me).wait_send()
        seven = w_ref.at[pl.ds(0, 7), c, 0]
        remote(seven, seven, ws.at[c], wr.at[c], me).wait_send()
        remote(seven, seven, wfs.at[c], wfr.at[c], me).wait_send()


def on_device(
    queries, query_gain, keys, values, out_weight, gate, doc_images, image_owner, image_start
):
    vmem = pl.BlockSpec(memory_space=pltpu.VMEM)
    smem = pl.BlockSpec(memory_space=pltpu.SMEM)
    hbm = pl.BlockSpec(memory_space=pl.ANY)
    bf16, f32 = jnp.bfloat16, jnp.float32
    dma = pltpu.SemaphoreType.DMA
    out = pl.pallas_call(
        kernel,
        out_shape=jax.ShapeDtypeStruct((2, PEERS, ROWS, 128), bf16),
        in_specs=[vmem, vmem, hbm, hbm, hbm, smem, smem, smem, smem],
        out_specs=vmem,
        scratch_shapes=[
            pltpu.VMEM((TOK, 256), bf16),
            pltpu.VMEM((TOK, 256), bf16),
            pltpu.VMEM((2, HD, BODY + 128), bf16),
            pltpu.VMEM((2, 128, HD), bf16),
            pltpu.VMEM((PEERS, CHUNKS, 2, 256, 128), bf16),
            pltpu.VMEM((CHUNKS, PLANES, ROWS, WIDE), bf16),
            pltpu.VMEM((CHUNKS, PEERS, ROWS, WIDE), bf16),
            pltpu.VMEM((CHUNKS, PEERS, ROWS, WIDE), bf16),
            pltpu.VMEM((CHUNKS, PEERS, ROWS, BLOCK), bf16),
            pltpu.VMEM((CHUNKS, PEERS, ROWS, BLOCK), bf16),
            pltpu.VMEM((CHUNKS, PLANES, ROWS, BLOCK), bf16),
            pltpu.VMEM((CHUNKS, PLANES, ROWS, BLOCK), bf16),
            pltpu.VMEM((CHUNKS, PLANES, ROWS, WIDE), bf16),
            pltpu.VMEM((PLANES * ROWS, PEERS * 128), f32),
            pltpu.VMEM((4, PEERS, 2, ROWS, 128), bf16),
            pltpu.VMEM((4 * PEERS, 2, ROWS, 128), bf16),
            dma(()), dma(()), dma(()),
        ]
        + [dma((CHUNKS,))] * 14
        + [dma(()), dma(())],
        compiler_params=pltpu.CompilerParams(
            collective_id=0, has_side_effects=True, vmem_limit_bytes=60 << 20
        ),
    )(
        queries, query_gain.reshape(1, HD), keys, values,
        out_weight.reshape(CHUNKS, 2, 256, 128), gate, doc_images, image_owner, image_start,
    )
    return out.reshape(256, 128)


def solution(mesh):
    placed = (
        P("image", "tensor"),
        P(),
        P("image", None, "tensor"),
        P("image", None, "tensor"),
        P("tensor", "image"),
        P(),
        P(),
        P(),
        P(),
    )
    return jax.shard_map(
        on_device, mesh=mesh, in_specs=placed, out_specs=P("tensor", "image"), check_vma=False
    )
```

```python
import functools
import math

import jax
import jax.numpy as jnp
from jax import lax
from jax.experimental import pallas as pl
from jax.experimental.pallas import tpu as pltpu
from jax.sharding import PartitionSpec as P

HD = 128
ROWS = 16
PLANES = 8
PEERS = 8
CHUNKS = 4
HEADS = 4
WIDE = HEADS * HD
TOK = 6404
BODY = 6400
NONE = -1e30
SEEN = -1e29
MESH = pl.DeviceIdType.MESH
NT = (((1,), (1,)), ((), ()))
FAR = (4, 3, 5, 2, 6, 1, 7)


def kernel(
    q_ref, gain_ref, k_hbm, v_hbm, w_hbm, gate_ref, docs_ref, owner_ref, start_ref,
    out_ref,
    k_ref, v_ref, vt_ref, kt_ref, w_ref,
    q1, sel, q2, obuf, m3, dbuf, m4, ostat, m3stat, dstat, m4stat, ag, part, partb, rs,
    ksem, vsem, wsem,
    s1s, s1r, s2s, s2r, s3s, s3r, s4s, s4r, s5s, s5r, ws, wr, wfs, wfr, t3s, t3r, t4s, t4r, s7s, s7r,
):
    me = lax.axis_index("image")
    y = lax.axis_index("tensor")
    z, p = me // PEERS, lax.rem(me, PEERS)
    x, core = p // 2, lax.rem(p, 2)
    other = 1 - core

    def image_id(zz, pp):
        return zz * PEERS + pp

    def remote(src, dst, ssem, rsem, img, yy=None):
        return pltpu.make_async_remote_copy(
            src_ref=src, dst_ref=dst, send_sem=ssem, recv_sem=rsem,
            device_id=(img, y if yy is None else yy), device_id_type=MESH,
        )

    k_copy = pltpu.make_async_copy(k_hbm.at[0], k_ref, ksem)
    v_copy = pltpu.make_async_copy(v_hbm.at[0], v_ref, vsem)
    w_copy = pltpu.make_async_copy(w_hbm, w_ref.at[p], wsem)
    v_copy.start()
    k_copy.start()
    w_copy.start()

    barrier = pltpu.get_barrier_semaphore()

    def greet(img, yy):
        pl.semaphore_signal(barrier, inc=1, device_id=(img, yy), device_id_type=MESH)

    for j in range(1, PLANES):
        greet(image_id(lax.rem(z + j, PLANES), p), y)
    for j in range(4):
        for d in range(PEERS):
            if j or d:
                greet(image_id(z, lax.rem(p + d, PEERS)), lax.rem(y + j, 4))

    gain = gain_ref[...].astype(jnp.float32) * (math.log2(math.e) / math.sqrt(HD))
    for h in range(CHUNKS * HEADS):
        rows = q_ref[:, h * HD : (h + 1) * HD].astype(jnp.float32)
        inv = lax.rsqrt(jnp.mean(rows * rows, axis=1, keepdims=True) + 1e-05)
        lo = (h % HEADS) * HD
        q1[h // HEADS, 0, :, lo : lo + HD] = (rows * inv * gain).astype(jnp.bfloat16)

    pl.semaphore_wait(barrier, 38)

    for c in range(CHUNKS):
        for j in FAR:
            remote(
                q1.at[c, 0], q1.at[c, j], s1s.at[c], s1r.at[c],
                image_id(lax.rem(z + j, PLANES), p),
            ).start()
    sibling = image_id(z, x * 2 + other)

    def send_weight(c, steps):
        for step in steps:
            for e in range(2):
                pp = lax.rem(x + step, 4) * 2 + e
                remote(
                    w_hbm.at[c, e], w_ref.at[p, c, e], ws.at[c], wr.at[c], image_id(z, pp)
                ).start()

    def near_weight(c):
        remote(
            w_hbm.at[c, other], w_ref.at[p, c, other], ws.at[c], wr.at[c], sibling
        ).start()
        send_weight(c, (1, 3))

    def far_weight(c):
        send_weight(c, (2,))

    def pass_weight(c):
        seven = w_ref.at[pl.ds(0, 7), c, core]
        remote(seven, seven, ws.at[c], wr.at[c], me).wait_recv()
        for d in range(2, PEERS, 2):
            block = w_ref.at[lax.rem(p + d, PEERS), c, core]
            remote(block, block, wfs.at[c], wfr.at[c], sibling).start()
        for d in range(2, PEERS, 2):
            block = w_ref.at[lax.rem(x * 2 + other + d, PEERS), c, core]
            remote(block, block, wfs.at[c], wfr.at[c], sibling).start()
        block = w_hbm.at[c, core]
        remote(block, w_ref.at[p, c, core], wfs.at[c], wfr.at[c], sibling).start()

    near_weight(0)
    far_weight(0)

    def scan_images(i, carry):
        doc, end, begin, found = carry
        step = (i >= end).astype(jnp.int32)
        doc = doc + step
        end = end + step * docs_ref[jnp.minimum(doc, PLANES - 1)]
        slot = owner_ref[i]
        begin = jnp.where(slot == me, start_ref[i], begin)
        found = tuple(
            jnp.where(slot == image_id(z, lax.rem(p + d, PEERS)), doc, found[d])
            for d in range(PEERS)
        )
        return doc, end, begin, found

    zero = jnp.int32(0)
    _, _, begin, doc_of = lax.fori_loop(
        0, owner_ref.shape[0], scan_images, (zero, docs_ref[0], zero, (zero,) * PEERS)
    )

    def stage2(c):
        remote(q1.at[c, pl.ds(1, 7)], q1.at[c, pl.ds(1, 7)], s1s.at[c], s1r.at[c], me).wait_recv()
        planes = [q1[c, j] for j in range(PLANES)]
        docs = [lax.rem(z - j + PLANES, PLANES) for j in range(PLANES)]
        for d in FAR + (0,):
            rows = planes[0]
            for j in range(1, PLANES):
                rows = jnp.where(doc_of[d] == docs[j], planes[j], rows)
            if d == 0:
                q2[c, 0] = rows
            else:
                sel[c, d] = rows
                remote(
                    sel.at[c, d], q2.at[c, d], s2s.at[c], s2r.at[c],
                    image_id(z, lax.rem(p + d, PEERS)),
                ).start()

    def attention(c):
        lanes = pl.ds(pl.multiple_of((c // 2) * HD, HD), HD)
        remote(q2.at[c, pl.ds(1, 7)], q2.at[c, pl.ds(1, 7)], s2s.at[c], s2r.at[c], me).wait_recv()
        rows = q2[c].reshape(PEERS * ROWS, WIDE)
        rows = jnp.concatenate([rows[:, r * HD : (r + 1) * HD] for r in range(HEADS)], axis=0)
        s = lax.dot_general(k_ref[0:BODY, lanes], rows, NT, preferred_element_type=jnp.float32)
        st = lax.dot_general(kt_ref[c // 2], rows, NT, preferred_element_type=jnp.float32)
        token = lax.broadcasted_iota(jnp.int32, st.shape, 0)
        st = jnp.where(token < TOK - BODY, st, NONE)
        peak = jnp.maximum(jnp.max(s, axis=0, keepdims=True), jnp.max(st, axis=0, keepdims=True))
        w = jnp.exp2(s - peak)
        wt = jnp.exp2(st - peak)
        acc = jnp.dot(
            vt_ref[c // 2, :, 0:BODY], w.astype(jnp.bfloat16), preferred_element_type=jnp.float32
        ) + jnp.dot(
            vt_ref[c // 2, :, BODY : BODY + 128], wt.astype(jnp.bfloat16),
            preferred_element_type=jnp.float32,
        )
        total = jnp.sum(w, axis=0, keepdims=True) + jnp.sum(wt, axis=0, keepdims=True)
        acc = acc * (1.0 / total)
        lse = peak + jnp.log2(total)
        place = lax.rem(lax.broadcasted_iota(jnp.int32, lse.shape, 1), HD)
        position = lax.rem(p - place // ROWS + PEERS, PEERS) * ROWS + lax.rem(place, ROWS)
        lse = jnp.where(position >= begin, lse, NONE)
        stat = jnp.zeros((PEERS, 128), jnp.float32)
        for r in range(HEADS):
            row = jnp.broadcast_to(lse[:, r * HD : (r + 1) * HD], (PEERS, 128))
            for d in range(PEERS):
                here = jnp.logical_and(slot_of == d, head_of == r)
                stat = jnp.where(here, pltpu.roll(row, (r - d) * ROWS % 128, 1), stat)
        for r in range(HEADS):
            rows = acc[:, r * HD : (r + 1) * HD].T.astype(jnp.bfloat16)
            rows = rows.reshape(PEERS, ROWS, HD)
            obuf[c, :, :, r * HD : (r + 1) * HD] = rows
            m3[c, 0, :, r * HD : (r + 1) * HD] = rows[0]
        for d in range(PEERS):
            ostat[c, d] = stat[d : d + 1]
        m3stat[c, 0] = stat[0:1]
        for d in FAR:
            target = image_id(z, lax.rem(p - d + PEERS, PEERS))
            remote(obuf.at[c, d], m3.at[c, d], s3s.at[c], s3r.at[c], target).start()
            remote(ostat.at[c, d], m3stat.at[c, d], t3s.at[c], t3r.at[c], target).start()

    def spread(factor, d):
        return jnp.concatenate(
            [
                jnp.broadcast_to(factor[r * ROWS : (r + 1) * ROWS, d : d + 1], (ROWS, HD))
                for r in range(HEADS)
            ],
            axis=1,
        )

    def combine(stat, member):
        member = jnp.logical_and(member, stat > SEEN)
        top = jnp.max(jnp.where(member, stat, NONE), axis=0, keepdims=True)
        weight = jnp.where(member, jnp.exp2(stat - top), 0.0)
        total = jnp.sum(weight, axis=0, keepdims=True)
        some = total > 0.0
        safe = jnp.where(some, total, 1.0)
        return weight * (1.0 / safe), jnp.where(some, top + jnp.log2(safe), NONE)

    def turned(factor):
        return jnp.concatenate([factor, jnp.zeros((120, 128), jnp.float32)], axis=0).T

    slot_of = lax.broadcasted_iota(jnp.int32, (PEERS, 128), 0)
    head_of = lax.broadcasted_iota(jnp.int32, (PEERS, 128), 1) // ROWS
    doc_rows = jnp.zeros((PEERS, 128), jnp.int32)
    for d in range(PEERS):
        doc_rows = jnp.where(slot_of == d, doc_of[d], doc_rows)

    def stage4(c):
        remote(m3.at[c, pl.ds(1, 7)], m3.at[c, pl.ds(1, 7)], s3s.at[c], s3r.at[c], me).wait_recv()
        seven = m3stat.at[c, pl.ds(1, 7)]
        remote(seven, seven, t3s.at[c], t3r.at[c], me).wait_recv()
        stat = jnp.concatenate([m3stat[c, d] for d in range(PEERS)], axis=0)
        factor = jnp.zeros((PEERS, 128), jnp.float32)
        for j in range(PLANES):
            doc = lax.rem(z + j, PLANES)
            weight, lse = combine(stat, doc_rows == doc)
            factor += weight
            dstat[c, j] = lse
        factor = turned(factor)
        scaled = [m3[c, d].astype(jnp.float32) * spread(factor, d) for d in range(PEERS)]
        for j in FAR + (0,):
            doc = lax.rem(z + j, PLANES)
            rows = functools.reduce(
                jnp.add, [jnp.where(doc_of[d] == doc, scaled[d], 0.0) for d in range(PEERS)]
            ).astype(jnp.bfloat16)
            if j == 0:
                m4[c, 0] = rows
                m4stat[c, 0] = dstat[c, 0]
            else:
                dbuf[c, j] = rows
                target = image_id(lax.rem(z + j, PLANES), p)
                remote(dbuf.at[c, j], m4.at[c, j], s4s.at[c], s4r.at[c], target).start()
                remote(dstat.at[c, j], m4stat.at[c, j], t4s.at[c], t4r.at[c], target).start()

    def stage5(c):
        remote(m4.at[c, pl.ds(1, 7)], m4.at[c, pl.ds(1, 7)], s4s.at[c], s4r.at[c], me).wait_recv()
        seven = m4stat.at[c, pl.ds(1, 7)]
        remote(seven, seven, t4s.at[c], t4r.at[c], me).wait_recv()
        stat = jnp.concatenate([m4stat[c, j] for j in range(PLANES)], axis=0)
        factor, _ = combine(stat, stat > SEEN)
        factor = turned(factor)
        rows = functools.reduce(
            jnp.add,
            [m4[c, j].astype(jnp.float32) * spread(factor, j) for j in range(PLANES)],
        ).astype(jnp.bfloat16)
        ag[c, 0] = rows
        for j in FAR:
            remote(
                ag.at[c, 0], ag.at[c, j], s5s.at[c], s5r.at[c],
                image_id(lax.rem(z + j, PLANES), p),
            ).start()

    def project(c):
        seven = ag.at[c, pl.ds(1, 7)]
        remote(seven, seven, s5s.at[c], s5r.at[c], me).wait_recv()
        seven = w_ref.at[pl.ds(0, 7), c, other]
        remote(seven, seven, wfs.at[c], wfr.at[c], me).wait_recv()
        rows = ag[c].reshape(PLANES * ROWS, WIDE)
        for d in range(PEERS):
            cols = slice(d * 128, (d + 1) * 128)
            part[:, cols] += jnp.dot(
                rows, w_ref[d, c].reshape(WIDE, 128), preferred_element_type=jnp.float32
            )

    stage2(0)
    part[...] = jnp.zeros_like(part)
    v_copy.wait()

    def turn(i, unused):
        body = pl.ds(pl.multiple_of(i * 1280, 1280), 1280)
        for g in range(2):
            vt_ref[g, :, body] = v_ref[body, g * HD : (g + 1) * HD].T
        return unused

    lax.fori_loop(0, BODY // 1280, turn, 0)
    k_copy.wait()
    pad = jnp.zeros((128 - (TOK - BODY), HD), jnp.bfloat16)
    for g in range(2):
        lanes = slice(g * HD, (g + 1) * HD)
        vt_ref[g, :, BODY : BODY + 128] = jnp.concatenate([v_ref[BODY:TOK, lanes], pad], axis=0).T
        kt_ref[g] = jnp.concatenate([k_ref[BODY:TOK, lanes], pad], axis=0)
    w_copy.wait()

    def turn_of(t, unused):
        def at(first, last, stage, *args):
            @pl.when(jnp.logical_and(t >= first, t <= last))
            def _():
                stage(*args)

        at(0, 2, stage2, t + 1)
        at(0, 0, near_weight, 1)
        at(1, 1, far_weight, 1)
        at(2, 2, near_weight, 2)
        at(0, 3, attention, t)
        at(3, 3, far_weight, 2)
        at(3, 3, near_weight, 3)
        at(3, 3, far_weight, 3)
        at(1, 3, stage4, t - 1)
        at(2, 3, stage5, t - 2)
        at(2, 2, pass_weight, t - 2)
        return unused

    lax.fori_loop(0, CHUNKS, turn_of, 0)
    stage4(3)
    pass_weight(1)
    stage5(2)
    project(0)
    pass_weight(2)
    project(1)
    stage5(3)
    pass_weight(3)
    project(2)
    project(3)

    for j in (2, 1, 3, 0):
        yy = lax.rem(y + j, 4)
        for e in range(2):
            slot = lax.rem(z - (2 * yy + e) + PLANES, PLANES)
            rows = part[pl.ds(pl.multiple_of(slot * ROWS, ROWS), ROWS), :].astype(jnp.bfloat16)
            for d in range(PEERS):
                partb[j, d, e] = rows[:, d * 128 : (d + 1) * 128]
        for d in FAR + (0,):
            if j or d:
                pp = lax.rem(p + d, PEERS)
                remote(partb.at[j, pp], rs.at[8 * j + d], s7s, s7r, image_id(z, pp), yy).start()
    most = rs.at[pl.ds(1, 31)]
    remote(most, most, s7s, s7r, me).wait()
    gate = jnp.tanh(jnp.full((8, 128), gate_ref[0], jnp.float32))[0:1]
    rs[0] = partb[0, p]
    for d in range(PEERS):
        total = rs[d].astype(jnp.float32)
        for j in range(1, 4):
            total += rs[8 * j + d].astype(jnp.float32)
        out_ref[:, lax.rem(p - d + PEERS, PEERS)] = (gate * total).astype(jnp.bfloat16)

    for c in range(CHUNKS):
        for buf, sems in (
            (q1, s1s), (sel, s2s), (obuf, s3s), (dbuf, s4s), (ag, s5s),
            (ostat, t3s), (dstat, t4s),
        ):
            seven = buf.at[c, pl.ds(1, 7)]
            remote(seven, seven, sems.at[c], s1r.at[c], me).wait_send()
        seven = w_ref.at[pl.ds(0, 7), c, 0]
        remote(seven, seven, ws.at[c], wr.at[c], me).wait_send()
        remote(seven, seven, wfs.at[c], wfr.at[c], me).wait_send()


def on_device(
    queries, query_gain, keys, values, out_weight, gate, doc_images, image_owner, image_start
):
    vmem = pl.BlockSpec(memory_space=pltpu.VMEM)
    smem = pl.BlockSpec(memory_space=pltpu.SMEM)
    hbm = pl.BlockSpec(memory_space=pl.ANY)
    bf16, f32 = jnp.bfloat16, jnp.float32
    dma = pltpu.SemaphoreType.DMA
    out = pl.pallas_call(
        kernel,
        out_shape=jax.ShapeDtypeStruct((2, PEERS, ROWS, 128), bf16),
        in_specs=[vmem, vmem, hbm, hbm, hbm, smem, smem, smem, smem],
        out_specs=vmem,
        scratch_shapes=[
            pltpu.VMEM((TOK, 256), bf16),
            pltpu.VMEM((TOK, 256), bf16),
            pltpu.VMEM((2, HD, BODY + 128), bf16),
            pltpu.VMEM((2, 128, HD), bf16),
            pltpu.VMEM((PEERS, CHUNKS, 2, 256, 128), bf16),
            pltpu.VMEM((CHUNKS, PLANES, ROWS, WIDE), bf16),
            pltpu.VMEM((CHUNKS, PEERS, ROWS, WIDE), bf16),
            pltpu.VMEM((CHUNKS, PEERS, ROWS, WIDE), bf16),
            pltpu.VMEM((CHUNKS, PEERS, ROWS, WIDE), bf16),
            pltpu.VMEM((CHUNKS, PEERS, ROWS, WIDE), bf16),
            pltpu.VMEM((CHUNKS, PLANES, ROWS, WIDE), bf16),
            pltpu.VMEM((CHUNKS, PLANES, ROWS, WIDE), bf16),
            pltpu.VMEM((CHUNKS, PEERS, 1, 128), f32),
            pltpu.VMEM((CHUNKS, PEERS, 1, 128), f32),
            pltpu.VMEM((CHUNKS, PLANES, 1, 128), f32),
            pltpu.VMEM((CHUNKS, PLANES, 1, 128), f32),
            pltpu.VMEM((CHUNKS, PLANES, ROWS, WIDE), bf16),
            pltpu.VMEM((PLANES * ROWS, PEERS * 128), f32),
            pltpu.VMEM((4, PEERS, 2, ROWS, 128), bf16),
            pltpu.VMEM((4 * PEERS, 2, ROWS, 128), bf16),
            dma(()), dma(()), dma(()),
        ]
        + [dma((CHUNKS,))] * 18
        + [dma(()), dma(())],
        compiler_params=pltpu.CompilerParams(
            collective_id=0, has_side_effects=True, vmem_limit_bytes=60 << 20
        ),
    )(
        queries, query_gain.reshape(1, HD), keys, values,
        out_weight.reshape(CHUNKS, 2, 256, 128), gate, doc_images, image_owner, image_start,
    )
    return out.reshape(256, 128)


def solution(mesh):
    placed = (
        P("image", "tensor"),
        P(),
        P("image", None, "tensor"),
        P("image", None, "tensor"),
        P("tensor", "image"),
        P(),
        P(),
        P(),
        P(),
    )
    return jax.shard_map(
        on_device, mesh=mesh, in_specs=placed, out_specs=P("tensor", "image"), check_vma=False
    )
```

```python
import functools
import math

import jax
import jax.numpy as jnp
from jax import lax
from jax.experimental import pallas as pl
from jax.experimental.pallas import tpu as pltpu
from jax.sharding import PartitionSpec as P

HD = 128
ROWS = 16
PLANES = 8
PEERS = 8
CHUNKS = 4
HEADS = 4
WIDE = HEADS * HD
TOK = 6404
BODY = 6400
NONE = -1e30
SEEN = -1e29
MESH = pl.DeviceIdType.MESH
NT = (((1,), (1,)), ((), ()))
FAR = (4, 3, 5, 2, 6, 1, 7)


def kernel(
    q_ref, gain_ref, k_hbm, v_hbm, w_hbm, docs_ref, owner_ref, start_ref,
    out_ref,
    k_ref, v_ref, vt_ref, kt_ref, w_ref,
    q1, sel, q2, obuf, m3, dbuf, m4, ostat, m3stat, dstat, m4stat, ag, part, partb, rs,
    ksem, vsem, wsem,
    s1s, s1r, s2s, s2r, s3s, s3r, s4s, s4r, s5s, s5r, ws, wr, wfs, wfr, t3s, t3r, t4s, t4r, s7s, s7r,
):
    me = lax.axis_index("image")
    y = lax.axis_index("tensor")
    z, p = me // PEERS, lax.rem(me, PEERS)
    x, core = p // 2, lax.rem(p, 2)
    other = 1 - core

    def image_id(zz, pp):
        return zz * PEERS + pp

    def remote(src, dst, ssem, rsem, img, yy=None):
        return pltpu.make_async_remote_copy(
            src_ref=src, dst_ref=dst, send_sem=ssem, recv_sem=rsem,
            device_id=(img, y if yy is None else yy), device_id_type=MESH,
        )

    k_copy = pltpu.make_async_copy(k_hbm.at[0], k_ref, ksem)
    v_copy = pltpu.make_async_copy(v_hbm.at[0], v_ref, vsem)
    w_copy = pltpu.make_async_copy(w_hbm, w_ref.at[p], wsem)
    v_copy.start()
    k_copy.start()
    w_copy.start()

    barrier = pltpu.get_barrier_semaphore()

    def greet(img, yy):
        pl.semaphore_signal(barrier, inc=1, device_id=(img, yy), device_id_type=MESH)

    for j in range(1, PLANES):
        greet(image_id(lax.rem(z + j, PLANES), p), y)
    for j in range(4):
        for d in range(PEERS):
            if j or d:
                greet(image_id(z, lax.rem(p + d, PEERS)), lax.rem(y + j, 4))

    gain = gain_ref[...].astype(jnp.float32) * (math.log2(math.e) / math.sqrt(HD))
    for h in range(CHUNKS * HEADS):
        rows = q_ref[:, h * HD : (h + 1) * HD].astype(jnp.float32)
        inv = lax.rsqrt(jnp.mean(rows * rows, axis=1, keepdims=True) + 1e-05)
        lo = (h % HEADS) * HD
        q1[h // HEADS, 0, :, lo : lo + HD] = (rows * inv * gain).astype(jnp.bfloat16)

    pl.semaphore_wait(barrier, 38)

    for c in range(CHUNKS):
        for j in FAR:
            remote(
                q1.at[c, 0], q1.at[c, j], s1s.at[c], s1r.at[c],
                image_id(lax.rem(z + j, PLANES), p),
            ).start()
    sibling = image_id(z, x * 2 + other)

    def send_weight(c, steps):
        for step in steps:
            for e in range(2):
                pp = lax.rem(x + step, 4) * 2 + e
                remote(
                    w_hbm.at[c, e], w_ref.at[p, c, e], ws.at[c], wr.at[c], image_id(z, pp)
                ).start()

    def near_weight(c):
        remote(
            w_hbm.at[c, other], w_ref.at[p, c, other], ws.at[c], wr.at[c], sibling
        ).start()
        send_weight(c, (1, 3))

    def far_weight(c):
        send_weight(c, (2,))

    def pass_weight(c):
        seven = w_ref.at[pl.ds(0, 7), c, core]
        remote(seven, seven, ws.at[c], wr.at[c], me).wait_recv()
        for d in range(2, PEERS, 2):
            block = w_ref.at[lax.rem(p + d, PEERS), c, core]
            remote(block, block, wfs.at[c], wfr.at[c], sibling).start()
        for d in range(2, PEERS, 2):
            block = w_ref.at[lax.rem(x * 2 + other + d, PEERS), c, core]
            remote(block, block, wfs.at[c], wfr.at[c], sibling).start()
        block = w_hbm.at[c, core]
        remote(block, w_ref.at[p, c, core], wfs.at[c], wfr.at[c], sibling).start()

    near_weight(0)
    far_weight(0)

    def scan_images(i, carry):
        doc, end, begin, found = carry
        step = (i >= end).astype(jnp.int32)
        doc = doc + step
        end = end + step * docs_ref[jnp.minimum(doc, PLANES - 1)]
        slot = owner_ref[i]
        begin = jnp.where(slot == me, start_ref[i], begin)
        found = tuple(
            jnp.where(slot == image_id(z, lax.rem(p + d, PEERS)), doc, found[d])
            for d in range(PEERS)
        )
        return doc, end, begin, found

    zero = jnp.int32(0)
    _, _, begin, doc_of = lax.fori_loop(
        0, owner_ref.shape[0], scan_images, (zero, docs_ref[0], zero, (zero,) * PEERS)
    )

    def stage2(c):
        remote(q1.at[c, pl.ds(1, 7)], q1.at[c, pl.ds(1, 7)], s1s.at[c], s1r.at[c], me).wait_recv()
        planes = [q1[c, j] for j in range(PLANES)]
        docs = [lax.rem(z - j + PLANES, PLANES) for j in range(PLANES)]
        for d in FAR + (0,):
            rows = planes[0]
            for j in range(1, PLANES):
                rows = jnp.where(doc_of[d] == docs[j], planes[j], rows)
            if d == 0:
                q2[c, 0] = rows
            else:
                sel[c, d] = rows
                remote(
                    sel.at[c, d], q2.at[c, d], s2s.at[c], s2r.at[c],
                    image_id(z, lax.rem(p + d, PEERS)),
                ).start()

    def attention(c):
        lanes = pl.ds(pl.multiple_of((c // 2) * HD, HD), HD)
        remote(q2.at[c, pl.ds(1, 7)], q2.at[c, pl.ds(1, 7)], s2s.at[c], s2r.at[c], me).wait_recv()
        rows = q2[c].reshape(PEERS * ROWS, WIDE)
        rows = jnp.concatenate([rows[:, r * HD : (r + 1) * HD] for r in range(HEADS)], axis=0)
        s = lax.dot_general(k_ref[0:BODY, lanes], rows, NT, preferred_element_type=jnp.float32)
        st = lax.dot_general(kt_ref[c // 2], rows, NT, preferred_element_type=jnp.float32)
        token = lax.broadcasted_iota(jnp.int32, st.shape, 0)
        st = jnp.where(token < TOK - BODY, st, NONE)
        peak = jnp.maximum(jnp.max(s, axis=0, keepdims=True), jnp.max(st, axis=0, keepdims=True))
        w = jnp.exp2(s - peak)
        wt = jnp.exp2(st - peak)
        acc = jnp.dot(
            vt_ref[c // 2, :, 0:BODY], w.astype(jnp.bfloat16), preferred_element_type=jnp.float32
        ) + jnp.dot(
            vt_ref[c // 2, :, BODY : BODY + 128], wt.astype(jnp.bfloat16),
            preferred_element_type=jnp.float32,
        )
        total = jnp.sum(w, axis=0, keepdims=True) + jnp.sum(wt, axis=0, keepdims=True)
        acc = acc * (1.0 / total)
        lse = peak + jnp.log2(total)
        place = lax.rem(lax.broadcasted_iota(jnp.int32, lse.shape, 1), HD)
        position = lax.rem(p - place // ROWS + PEERS, PEERS) * ROWS + lax.rem(place, ROWS)
        lse = jnp.where(position >= begin, lse, NONE)
        stat = jnp.zeros((PEERS, 128), jnp.float32)
        for r in range(HEADS):
            row = jnp.broadcast_to(lse[:, r * HD : (r + 1) * HD], (PEERS, 128))
            for d in range(PEERS):
                here = jnp.logical_and(slot_of == d, head_of == r)
                stat = jnp.where(here, pltpu.roll(row, (r - d) * ROWS % 128, 1), stat)
        for r in range(HEADS):
            rows = acc[:, r * HD : (r + 1) * HD].T.astype(jnp.bfloat16)
            rows = rows.reshape(PEERS, ROWS, HD)
            obuf[c, :, :, r * HD : (r + 1) * HD] = rows
            m3[c, 0, :, r * HD : (r + 1) * HD] = rows[0]
        for d in range(PEERS):
            ostat[c, d] = stat[d : d + 1]
        m3stat[c, 0] = stat[0:1]
        for d in FAR:
            target = image_id(z, lax.rem(p - d + PEERS, PEERS))
            remote(obuf.at[c, d], m3.at[c, d], s3s.at[c], s3r.at[c], target).start()
            remote(ostat.at[c, d], m3stat.at[c, d], t3s.at[c], t3r.at[c], target).start()

    def spread(factor, d):
        return jnp.concatenate(
            [
                jnp.broadcast_to(factor[r * ROWS : (r + 1) * ROWS, d : d + 1], (ROWS, HD))
                for r in range(HEADS)
            ],
            axis=1,
        )

    def combine(stat, member):
        member = jnp.logical_and(member, stat > SEEN)
        top = jnp.max(jnp.where(member, stat, NONE), axis=0, keepdims=True)
        weight = jnp.where(member, jnp.exp2(stat - top), 0.0)
        total = jnp.sum(weight, axis=0, keepdims=True)
        some = total > 0.0
        safe = jnp.where(some, total, 1.0)
        return weight * (1.0 / safe), jnp.where(some, top + jnp.log2(safe), NONE)

    def turned(factor):
        return jnp.concatenate([factor, jnp.zeros((120, 128), jnp.float32)], axis=0).T

    slot_of = lax.broadcasted_iota(jnp.int32, (PEERS, 128), 0)
    head_of = lax.broadcasted_iota(jnp.int32, (PEERS, 128), 1) // ROWS
    doc_rows = jnp.zeros((PEERS, 128), jnp.int32)
    for d in range(PEERS):
        doc_rows = jnp.where(slot_of == d, doc_of[d], doc_rows)

    def stage4(c):
        remote(m3.at[c, pl.ds(1, 7)], m3.at[c, pl.ds(1, 7)], s3s.at[c], s3r.at[c], me).wait_recv()
        seven = m3stat.at[c, pl.ds(1, 7)]
        remote(seven, seven, t3s.at[c], t3r.at[c], me).wait_recv()
        stat = jnp.concatenate([m3stat[c, d] for d in range(PEERS)], axis=0)
        factor = jnp.zeros((PEERS, 128), jnp.float32)
        for j in range(PLANES):
            doc = lax.rem(z + j, PLANES)
            weight, lse = combine(stat, doc_rows == doc)
            factor += weight
            dstat[c, j] = lse
        factor = turned(factor)
        scaled = [m3[c, d].astype(jnp.float32) * spread(factor, d) for d in range(PEERS)]
        for j in FAR + (0,):
            doc = lax.rem(z + j, PLANES)
            rows = functools.reduce(
                jnp.add, [jnp.where(doc_of[d] == doc, scaled[d], 0.0) for d in range(PEERS)]
            ).astype(jnp.bfloat16)
            if j == 0:
                m4[c, 0] = rows
                m4stat[c, 0] = dstat[c, 0]
            else:
                dbuf[c, j] = rows
                target = image_id(lax.rem(z + j, PLANES), p)
                remote(dbuf.at[c, j], m4.at[c, j], s4s.at[c], s4r.at[c], target).start()
                remote(dstat.at[c, j], m4stat.at[c, j], t4s.at[c], t4r.at[c], target).start()

    def stage5(c):
        remote(m4.at[c, pl.ds(1, 7)], m4.at[c, pl.ds(1, 7)], s4s.at[c], s4r.at[c], me).wait_recv()
        seven = m4stat.at[c, pl.ds(1, 7)]
        remote(seven, seven, t4s.at[c], t4r.at[c], me).wait_recv()
        stat = jnp.concatenate([m4stat[c, j] for j in range(PLANES)], axis=0)
        factor, _ = combine(stat, stat > SEEN)
        factor = turned(factor)
        rows = functools.reduce(
            jnp.add,
            [m4[c, j].astype(jnp.float32) * spread(factor, j) for j in range(PLANES)],
        ).astype(jnp.bfloat16)
        ag[c, 0] = rows
        for j in FAR:
            remote(
                ag.at[c, 0], ag.at[c, j], s5s.at[c], s5r.at[c],
                image_id(lax.rem(z + j, PLANES), p),
            ).start()

    def project(c):
        seven = ag.at[c, pl.ds(1, 7)]
        remote(seven, seven, s5s.at[c], s5r.at[c], me).wait_recv()
        seven = w_ref.at[pl.ds(0, 7), c, other]
        remote(seven, seven, wfs.at[c], wfr.at[c], me).wait_recv()
        rows = ag[c].reshape(PLANES * ROWS, WIDE)
        for d in range(PEERS):
            cols = slice(d * 128, (d + 1) * 128)
            part[:, cols] += jnp.dot(
                rows, w_ref[d, c].reshape(WIDE, 128), preferred_element_type=jnp.float32
            )

    stage2(0)
    part[...] = jnp.zeros_like(part)
    v_copy.wait()

    def turn(i, unused):
        body = pl.ds(pl.multiple_of(i * 1280, 1280), 1280)
        for g in range(2):
            vt_ref[g, :, body] = v_ref[body, g * HD : (g + 1) * HD].T
        return unused

    lax.fori_loop(0, BODY // 1280, turn, 0)
    k_copy.wait()
    pad = jnp.zeros((128 - (TOK - BODY), HD), jnp.bfloat16)
    for g in range(2):
        lanes = slice(g * HD, (g + 1) * HD)
        vt_ref[g, :, BODY : BODY + 128] = jnp.concatenate([v_ref[BODY:TOK, lanes], pad], axis=0).T
        kt_ref[g] = jnp.concatenate([k_ref[BODY:TOK, lanes], pad], axis=0)
    w_copy.wait()

    def turn_of(t, unused):
        def at(first, last, stage, *args):
            @pl.when(jnp.logical_and(t >= first, t <= last))
            def _():
                stage(*args)

        at(0, 2, stage2, t + 1)
        at(0, 0, near_weight, 1)
        at(1, 1, far_weight, 1)
        at(2, 2, near_weight, 2)
        at(0, 3, attention, t)
        at(3, 3, far_weight, 2)
        at(3, 3, near_weight, 3)
        at(3, 3, far_weight, 3)
        at(1, 3, stage4, t - 1)
        at(2, 3, stage5, t - 2)
        at(2, 2, pass_weight, t - 2)
        return unused

    lax.fori_loop(0, CHUNKS, turn_of, 0)
    stage4(3)
    pass_weight(1)
    stage5(2)
    project(0)
    pass_weight(2)
    project(1)
    stage5(3)
    pass_weight(3)
    project(2)
    project(3)

    for j in (2, 1, 3, 0):
        yy = lax.rem(y + j, 4)
        for e in range(2):
            slot = lax.rem(z - (2 * yy + e) + PLANES, PLANES)
            rows = part[pl.ds(pl.multiple_of(slot * ROWS, ROWS), ROWS), :].astype(jnp.bfloat16)
            for d in range(PEERS):
                partb[j, d, e] = rows[:, d * 128 : (d + 1) * 128]
        for d in FAR + (0,):
            if j or d:
                pp = lax.rem(p + d, PEERS)
                remote(partb.at[j, pp], rs.at[8 * j + d], s7s, s7r, image_id(z, pp), yy).start()
    most = rs.at[pl.ds(1, 31)]
    remote(most, most, s7s, s7r, me).wait()
    rs[0] = partb[0, p]
    for d in range(PEERS):
        total = rs[d].astype(jnp.float32)
        for j in range(1, 4):
            total += rs[8 * j + d].astype(jnp.float32)
        out_ref[:, lax.rem(p - d + PEERS, PEERS)] = total

    for c in range(CHUNKS):
        for buf, sems in (
            (q1, s1s), (sel, s2s), (obuf, s3s), (dbuf, s4s), (ag, s5s),
            (ostat, t3s), (dstat, t4s),
        ):
            seven = buf.at[c, pl.ds(1, 7)]
            remote(seven, seven, sems.at[c], s1r.at[c], me).wait_send()
        seven = w_ref.at[pl.ds(0, 7), c, 0]
        remote(seven, seven, ws.at[c], wr.at[c], me).wait_send()
        remote(seven, seven, wfs.at[c], wfr.at[c], me).wait_send()


def on_device(
    queries, query_gain, keys, values, out_weight, gate, doc_images, image_owner, image_start
):
    vmem = pl.BlockSpec(memory_space=pltpu.VMEM)
    smem = pl.BlockSpec(memory_space=pltpu.SMEM)
    hbm = pl.BlockSpec(memory_space=pl.ANY)
    bf16, f32 = jnp.bfloat16, jnp.float32
    dma = pltpu.SemaphoreType.DMA
    out = pl.pallas_call(
        kernel,
        out_shape=jax.ShapeDtypeStruct((2, PEERS, ROWS, 128), f32),
        in_specs=[vmem, vmem, hbm, hbm, hbm, smem, smem, smem],
        out_specs=vmem,
        scratch_shapes=[
            pltpu.VMEM((TOK, 256), bf16),
            pltpu.VMEM((TOK, 256), bf16),
            pltpu.VMEM((2, HD, BODY + 128), bf16),
            pltpu.VMEM((2, 128, HD), bf16),
            pltpu.VMEM((PEERS, CHUNKS, 2, 256, 128), bf16),
            pltpu.VMEM((CHUNKS, PLANES, ROWS, WIDE), bf16),
            pltpu.VMEM((CHUNKS, PEERS, ROWS, WIDE), bf16),
            pltpu.VMEM((CHUNKS, PEERS, ROWS, WIDE), bf16),
            pltpu.VMEM((CHUNKS, PEERS, ROWS, WIDE), bf16),
            pltpu.VMEM((CHUNKS, PEERS, ROWS, WIDE), bf16),
            pltpu.VMEM((CHUNKS, PLANES, ROWS, WIDE), bf16),
            pltpu.VMEM((CHUNKS, PLANES, ROWS, WIDE), bf16),
            pltpu.VMEM((CHUNKS, PEERS, 1, 128), f32),
            pltpu.VMEM((CHUNKS, PEERS, 1, 128), f32),
            pltpu.VMEM((CHUNKS, PLANES, 1, 128), f32),
            pltpu.VMEM((CHUNKS, PLANES, 1, 128), f32),
            pltpu.VMEM((CHUNKS, PLANES, ROWS, WIDE), bf16),
            pltpu.VMEM((PLANES * ROWS, PEERS * 128), f32),
            pltpu.VMEM((4, PEERS, 2, ROWS, 128), bf16),
            pltpu.VMEM((4 * PEERS, 2, ROWS, 128), bf16),
            dma(()), dma(()), dma(()),
        ]
        + [dma((CHUNKS,))] * 18
        + [dma(()), dma(())],
        compiler_params=pltpu.CompilerParams(
            collective_id=0, has_side_effects=True, vmem_limit_bytes=60 << 20
        ),
    )(
        queries, query_gain.reshape(1, HD), keys, values,
        out_weight.reshape(CHUNKS, 2, 256, 128), doc_images, image_owner, image_start,
    )
    return (jnp.tanh(gate[0]) * out.reshape(256, 128)).astype(bf16)


def solution(mesh):
    placed = (
        P("image", "tensor"),
        P(),
        P("image", None, "tensor"),
        P("image", None, "tensor"),
        P("tensor", "image"),
        P(),
        P(),
        P(),
        P(),
    )
    return jax.shard_map(
        on_device, mesh=mesh, in_specs=placed, out_specs=P("tensor", "image"), check_vma=False
    )
```
